512 devices in a mesh: leaf: 32 (over z, core), vec: 16 (over y, x).
Axes of the slice: x: 4, y: 4, z: 16, core: 2. Of those that a mesh axis runs over, the one named last changes fastest.
Arguments:
- points: bfloat16 [512, 3, 256], P('leaf'), may hold values from 0 to 1
- probe_vectors: bfloat16 [512, 256, 256], P('leaf', 'vec'), may hold values from -6 to 6
- neighbours: int32 [512, 16], P('leaf'), may hold values from -1 to 511, as said below
- leaf_pivots: int32 [512, 64], P('leaf'), may hold values from 0 to 255, as said below
- leaf_inverse: float32 [512, 64, 64], P('leaf'), as said below
- local_pivots: int32 [480, 64], P('leaf'), may hold values from 0 to 127, as said below
- local_inverse: float32 [480, 64, 64], P('leaf'), as said below
- upper_pivots: int32 [28, 64], replicated, may hold values from 0 to 127, as said below
- upper_inverse: float32 [28, 64, 64], replicated, as said below
Outputs:
- leaf_interp: float32 [512, 256, 64], P('leaf')
- local_interp: float32 [480, 128, 64], P('leaf')
- upper_interp: float32 [32, 3, 128, 64], P('leaf')
- top_sketch: float32 [32, 256, 64], P('leaf', 'vec')
The draws below stay inside these ranges and needn't reach their ends.
Inputs may be any that keep to these rules, and one draw needn't show every extreme that they name: Entry 0 of neighbours[i] is i; then come distinct clusters j != i with |j - i| <= 16, then -1 to the end. The first cluster of each group of 16 lists the cluster before it in entry 1, and the last one lists the cluster after it there, where those exist. A list holds at least 4 clusters, and some lists hold 16. `leaf_pivots`: each row holds 64 distinct row numbers. `local_pivots`: each row holds 64 distinct row numbers. `upper_pivots`: each row holds 64 distinct row numbers. `leaf_inverse`: diagonal entries lie in 0.5 to 1.5. `local_inverse`: diagonal entries lie in 0.5 to 1.5. `upper_inverse`: diagonal entries lie in 0.5 to 1.5.
All inputs are finite; a program needn't handle non-finite values.
Results may differ from the reference program's by a relative error of at most 0.0013.
Values may be sent and summed in bfloat16 or wider, within the bound.
A program may use at most 64 MiB of HBM per device.

```python
import jax
import jax.numpy as jnp
from jax import lax

P_SIZE = 256
K = 64
S = 256
NB = 16
LEVELS_LOCAL = 4
UPL = 3
LEAF_DEV = 16
CLUSTERS = 512
LOCAL_NODES = 480
UNODES = 28


def pivot_rows(key, node_count, row_total):
    scores = jax.random.randint(key, (node_count, row_total), 0, 2 ** 16) * row_total + jnp.arange(row_total, dtype=jnp.int32)[None, :]
    ranking = jnp.argsort(scores, axis=1)
    return ranking[:, :K].astype(jnp.int32)


def inverse_blocks(key, node_count):
    first_key, second_key = jax.random.split(key)
    diagonal = jax.random.uniform(first_key, (node_count, K), jnp.float32, 0.5, 1.5)
    off_part = jax.random.normal(second_key, (node_count, K, K), jnp.float32) * (0.3 / K ** 0.5)
    identity = jnp.eye(K, dtype=jnp.float32)
    return off_part * (1.0 - identity) + identity * diagonal[:, :, None]


def draw_neighbours(key, part):
    window = 2 * LEAF_DEV + 1
    offsets = jnp.arange(window, dtype=jnp.int32) - LEAF_DEV
    cluster = jnp.arange(CLUSTERS, dtype=jnp.int32)
    target = cluster[:, None] + offsets[None, :]
    in_range = (target >= 0) & (target < CLUSTERS) & (offsets[None, :] != 0)
    group_place = cluster % LEAF_DEV
    forced = jnp.where((group_place == 0) & (cluster > 0), cluster - 1, -1)
    forced = jnp.where((group_place == LEAF_DEV - 1) & (cluster < CLUSTERS - 1) & (forced < 0), cluster + 1, forced)
    first_key, second_key = jax.random.split(key)
    scores = jax.random.randint(first_key, (CLUSTERS, window), 0, 2 ** 16) * window + jnp.arange(window, dtype=jnp.int32)[None, :]
    scores = jnp.where(target == forced[:, None], -1, scores)
    scores = jnp.where(in_range, scores, 2 ** 30)
    ranking = jnp.argsort(scores, axis=1)[:, :NB - 1]
    chosen = jnp.take_along_axis(target, ranking, axis=1)
    counts = jax.random.randint(second_key, (CLUSTERS,), max(1, NB // 4), NB + 1)
    counts = jnp.where(cluster % 5 == 0, NB, counts)
    counts = jnp.where(forced >= 0, jnp.maximum(counts, 2), counts)
    slot_index = jnp.arange(NB - 1, dtype=jnp.int32)[None, :]
    listed = jnp.where(slot_index < counts[:, None] - 1, chosen, -1)
    return jnp.concatenate([cluster[:, None], listed], axis=1).astype(jnp.int32)


def draw_leaf_pivots(key, part):
    return pivot_rows(jax.random.fold_in(key, 11), CLUSTERS, P_SIZE)


def draw_local_pivots(key, part):
    return pivot_rows(jax.random.fold_in(key, 12), LOCAL_NODES, 2 * K)


def draw_upper_pivots(key, part):
    return pivot_rows(jax.random.fold_in(key, 13), UNODES, 2 * K)


def draw_leaf_inverse(key, part):
    return inverse_blocks(jax.random.fold_in(key, 21), CLUSTERS)


def draw_local_inverse(key, part):
    return inverse_blocks(jax.random.fold_in(key, 22), LOCAL_NODES)


def draw_upper_inverse(key, part):
    return inverse_blocks(jax.random.fold_in(key, 23), UNODES)


def level_of(rng, extent, shards, smallest, largest):
    def one(dim, shards_of):
        draws = jax.random.uniform(jax.random.fold_in(jax.random.fold_in(rng, 6), dim), (shards_of,), jnp.float32, smallest / len(shards), largest / len(shards))
        return jnp.repeat(jnp.exp(draws), extent[dim] // shards_of).reshape((-1,) + (1,) * (len(extent) - dim - 1))

    factor_of = one(*shards[0])
    for cut in shards[1:]:
        factor_of = factor_of * one(*cut)
    return factor_of


def gaussian(rng, extent, scale, limit, shards=(), kind=jnp.bfloat16):
    array = jax.random.normal(rng, extent, jnp.float32) * scale
    if len(shards) > 0:
        array = level_of(rng, extent, shards, -0.22, 0.18) * array
    return jnp.clip(array, min=-limit, max=limit).astype(kind)


def setup_inputs(seed: int = 0) -> dict:
    key_of = jax.random.split(jax.random.key(seed), 10)
    points = jnp.clip(1.0 * jax.random.uniform(key_of[0], (CLUSTERS, 3, P_SIZE), jnp.float32) ** level_of(key_of[0], (CLUSTERS, 3, P_SIZE), ((0, 32),), -0.2, 0.2), 0.0, 1.0).astype(jnp.bfloat16)
    probe_vectors = gaussian(key_of[1], (CLUSTERS, S, P_SIZE), 1.0, 6.0, ((0, 32), (1, 16)))
    neighbours = draw_neighbours(jax.random.fold_in(key_of[9], 71), 0)
    leaf_pivots = draw_leaf_pivots(jax.random.fold_in(key_of[9], 71), 0)
    leaf_inverse = draw_leaf_inverse(jax.random.fold_in(key_of[9], 71), 0)
    local_pivots = draw_local_pivots(jax.random.fold_in(key_of[9], 71), 0)
    local_inverse = draw_local_inverse(jax.random.fold_in(key_of[9], 71), 0)
    upper_pivots = draw_upper_pivots(jax.random.fold_in(key_of[9], 71), 0)
    upper_inverse = draw_upper_inverse(jax.random.fold_in(key_of[9], 71), 0)
    return {"points": points, "probe_vectors": probe_vectors, "neighbours": neighbours, "leaf_pivots": leaf_pivots, "leaf_inverse": leaf_inverse, "local_pivots": local_pivots, "local_inverse": local_inverse, "upper_pivots": upper_pivots, "upper_inverse": upper_inverse}


SOFTEN = 0.0009
EPSILON = 1e-06

def kernel_tile(near_points, far_points):
    near_xyz = near_points.astype(jnp.float32)
    far_xyz = far_points.astype(jnp.float32)
    distance = SOFTEN + jnp.zeros((near_xyz.shape[0], near_xyz.shape[2], far_xyz.shape[2]), jnp.float32)
    for coordinate in range(3):
        offset_gap = near_xyz[:, coordinate, :, None] - far_xyz[:, coordinate, None, :]
        distance = distance + offset_gap * offset_gap
    return 1.0 / (64.0 * jnp.sqrt(distance))

def interpolate(sketch, pivots, inverse, column_total):
    rows = sketch.shape[2]
    index_grid = jnp.broadcast_to(pivots[:, None, :], (sketch.shape[0], sketch.shape[1], pivots.shape[1]))
    chosen = jnp.take_along_axis(sketch, index_grid, axis=2)
    gram_rows = jnp.einsum('nsp,nsk->npk', sketch, chosen, precision=lax.Precision.HIGHEST)
    squares = lax.optimization_barrier(jnp.sum(sketch * sketch, axis=(1, 2)))
    mean_sq = squares / (rows * column_total) + EPSILON
    interp_map = jnp.einsum('npl,nlk->npk', gram_rows, inverse, precision=lax.Precision.HIGHEST)
    interp_map = interp_map / (column_total * mean_sq)[:, None, None]
    upward = jnp.einsum('nsp,npk->nsk', sketch, interp_map, precision=lax.Precision.HIGHEST)
    upward = upward / jnp.sqrt(mean_sq)[:, None, None]
    return (interp_map, upward)

def pair_children(upward):
    node_count = upward.shape[0] // 2
    paired = upward.reshape(node_count, 2, upward.shape[1], upward.shape[2])
    paired = jnp.transpose(paired, (0, 2, 1, 3))
    return paired.reshape(node_count, upward.shape[1], 2 * upward.shape[2])

def near_sketch(points, probe_vectors, neighbours):
    block_count = CLUSTERS // LEAF_DEV

    def one_block(inputs):
        block_points, block_lists = inputs

        def add_slot(slot_index, running):
            listed = lax.dynamic_slice_in_dim(block_lists, slot_index, 1, 1)[:, 0]
            present = listed >= 0
            safe_index = jnp.maximum(listed, 0).astype(jnp.int32)
            kernel_block = kernel_tile(block_points, points[safe_index])
            kernel_block = jnp.where(present[:, None, None], kernel_block, 0.0).astype(jnp.bfloat16)
            far_vectors = probe_vectors[safe_index].astype(jnp.float32)
            return running + jnp.einsum('nsq,npq->nsp', far_vectors, kernel_block.astype(jnp.float32))
        start = jnp.zeros((LEAF_DEV, S, P_SIZE), jnp.float32)
        return lax.fori_loop(0, NB, add_slot, start)
    result = lax.map(one_block, (points.reshape(block_count, LEAF_DEV, 3, P_SIZE), neighbours.reshape(block_count, LEAF_DEV, NB)))
    return result.reshape(CLUSTERS, S, P_SIZE)

def reference(points, probe_vectors, neighbours, leaf_pivots, leaf_inverse, local_pivots, local_inverse, upper_pivots, upper_inverse):
    sketch = near_sketch(points, probe_vectors, neighbours)
    leaf_interp, upward = interpolate(sketch, leaf_pivots, leaf_inverse, S)
    group_count = CLUSTERS // LEAF_DEV
    grouped_pivots = local_pivots.reshape(group_count, LEAF_DEV - 1, K)
    grouped_inverse = local_inverse.reshape(group_count, LEAF_DEV - 1, K, K)
    pieces = []
    offset = 0
    for tier_index in range(LEVELS_LOCAL):
        node_count = LEAF_DEV >> tier_index + 1
        node_pivots = grouped_pivots[:, offset:offset + node_count].reshape(-1, K)
        node_inverse = grouped_inverse[:, offset:offset + node_count].reshape(-1, K, K)
        interp_map, upward = interpolate(pair_children(upward), node_pivots, node_inverse, S)
        pieces.append(interp_map.reshape(group_count, node_count, 2 * K, K))
        offset = offset + node_count
    local_interp = jnp.concatenate(pieces, axis=1).reshape(group_count * (LEAF_DEV - 1), 2 * K, K)
    heap_offset = 0
    upper_maps = []
    for tier_index in range(UPL):
        node_count = group_count >> tier_index + 1
        interp_map, upward = interpolate(pair_children(upward), upper_pivots[heap_offset:heap_offset + node_count], upper_inverse[heap_offset:heap_offset + node_count], S)
        upper_maps.append(jnp.repeat(interp_map, 2 ** (tier_index + 1), axis=0))
        heap_offset = heap_offset + node_count
    upper_interp = jnp.stack(upper_maps, axis=1)
    top_sketch = jnp.repeat(upward, 2 ** UPL, axis=0)
    return (leaf_interp, local_interp, upper_interp, top_sketch)
```

```python
import functools

import jax
import jax.numpy as jnp
from jax import lax
from jax.experimental import pallas as pl
from jax.experimental.pallas import tpu as pltpu
from jax.sharding import PartitionSpec as P

UPL = 3
SOFTEN = 0.0009
EPSILON = 1e-06
F32 = jnp.float32
BF16 = jnp.bfloat16
NN = (((1,), (0,)), ((), ()))
NT = (((1,), (1,)), ((), ()))


def mm(a, b, dims=NN):
    return lax.dot_general(a, b, dims, preferred_element_type=F32)


def split(a):
    high = a.astype(BF16)
    return high, (a - high.astype(F32)).astype(BF16)


def mm3(a, b, dims=NN):
    return mm(a[0], b[0], dims) + (mm(a[0], b[1], dims) + mm(a[1], b[0], dims))


def feature_rows(xyz, weight):
    norm = SOFTEN / 2 + xyz[0] * xyz[0] + xyz[1] * xyz[1] + xyz[2] * xyz[2]
    high = norm.astype(BF16).astype(F32)
    rest = norm - high
    middle = rest.astype(BF16).astype(F32)
    low = (rest - middle).astype(BF16).astype(F32)
    return [part * weight for part in (high, middle, low)]


def body(
    leaf_n,
    vec_n,
    axes,
    pts,
    probe,
    nbr,
    leaf_piv,
    leaf_inv,
    local_piv,
    local_inv,
    upper_piv,
    upper_inv,
    out_leaf,
    out_local,
    out_upper,
    out_top,
    ext_pts,
    ext_probe,
    near,
    far,
    inv,
    weights,
    sketches,
    z_ref,
    joined,
    z_top,
    leaf_map,
    node_maps,
    inv_sem,
    own_sem,
    side_send,
    side_recv,
    sk_send,
    sk_recv,
    up_send,
    up_recv,
    map_send,
    map_recv,
    out_sem,
):
    leaf_axis, vec_axis = axes
    d = lax.axis_index(leaf_axis)
    v = lax.axis_index(vec_axis)
    levels = vec_n.bit_length() - 1
    columns = probe.shape[1]
    points = probe.shape[2]
    total = columns * vec_n

    def on_vec(u):
        return {leaf_axis: d, vec_axis: u}

    def on_leaf(g):
        return {leaf_axis: g, vec_axis: v}

    def remote(src, dst, send, recv, target):
        return pltpu.make_async_remote_copy(
            src_ref=src,
            dst_ref=dst,
            send_sem=send,
            recv_sem=recv,
            device_id=target,
            device_id_type=pl.DeviceIdType.MESH,
        )

    def flip(index, stride):
        return index + stride * (1 - 2 * ((index // stride) % 2))

    before = (d + leaf_n - 1) % leaf_n
    after = (d + 1) % leaf_n
    upper_partner = [flip(d, 1 << u) for u in range(UPL)]

    barrier = pltpu.get_barrier_semaphore()
    targets = [on_vec((v + t) % vec_n) for t in range(1, vec_n)]
    targets += [on_leaf(g) for g in [before, after] + upper_partner[1:]]
    for target in targets:
        pl.semaphore_signal(
            barrier, inc=1, device_id=target, device_id_type=pl.DeviceIdType.MESH
        )

    rows = [(leaf_piv, leaf_inv, v)]
    offset = 0
    for t in range(1, levels + 1):
        rows.append((local_piv, local_inv, offset + v // (1 << t)))
        offset += vec_n >> t
    offset = 0
    for u in range(1, UPL + 1):
        rows.append((upper_piv, upper_inv, offset + d // (1 << u)))
        offset += leaf_n >> u
    inv_copies = [
        pltpu.make_async_copy(source.at[row], inv.at[n], inv_sem.at[n])
        for n, (_, source, row) in enumerate(rows)
    ]
    for copy in inv_copies:
        copy.start()
    own_pts = pltpu.make_async_copy(pts, ext_pts.at[1], own_sem.at[0])
    own_probe = pltpu.make_async_copy(
        probe, ext_probe.at[pl.ds(vec_n, vec_n)], own_sem.at[1]
    )
    own_pts.start()
    own_probe.start()

    pl.semaphore_wait(barrier, len(targets))

    sides = []
    for n, (target, place) in enumerate([(after, 0), (before, 2)]):
        sides.append(
            remote(
                pts,
                ext_pts.at[place],
                side_send.at[2 * n],
                side_recv.at[2 * n],
                on_leaf(target),
            )
        )
        sides.append(
            remote(
                probe,
                ext_probe.at[pl.ds(place * vec_n, vec_n)],
                side_send.at[2 * n + 1],
                side_recv.at[2 * n + 1],
                on_leaf(target),
            )
        )
    for copy in sides:
        copy.start()

    for n, (pivots, _, row) in enumerate(rows):
        inv_copies[n].wait()
        size = points if n == 0 else 2 * inv.shape[1]
        chosen = pivots[pl.ds(row, 1), :]
        spread = (
            lax.broadcasted_iota(jnp.int32, (size, chosen.shape[1]), 0) == chosen
        ).astype(F32).astype(BF16)
        high, low = split(jnp.transpose(inv[n]))
        weights[n, 0, :, :size] = mm(high, spread, NT).astype(BF16)
        weights[n, 1, :, :size] = mm(low, spread, NT).astype(BF16)

    own_pts.wait()
    own_probe.wait()

    def features(side):
        xyz = [ext_pts[side, c].astype(F32) for c in range(3)]
        norm = feature_rows(xyz, 4096.0)
        one = jnp.ones((1, points), F32)
        pad = jnp.zeros((7, points), F32)
        for r in range(vec_n):
            at = [x[r : r + 1] for x in xyz]
            nm = [x[r : r + 1] for x in norm]
            if side == 1:
                near[r] = jnp.concatenate(at + nm + [one] * 3 + [pad], axis=0).astype(BF16)
            rows_far = [x * -8192.0 for x in at] + [one] * 3 + nm + [pad]
            far[side * vec_n + r] = jnp.transpose(
                jnp.concatenate(rows_far, axis=0)
            ).astype(BF16)

    features(1)
    for copy in sides[0:2]:
        copy.wait_recv()
    features(0)
    for copy in sides[2:4]:
        copy.wait_recv()
    features(2)

    first = (d - 1) * vec_n

    def sketch_of(c):
        near_c = near[c]

        def slot(k, acc):
            listed = nbr[c, k]
            place = jnp.clip(listed - first, 0, 3 * vec_n - 1)
            distance = mm(far[place], near_c)
            tile = lax.rsqrt(distance).astype(BF16)
            vectors = ext_probe[place]
            vectors = jnp.where(listed >= 0, vectors, jnp.zeros_like(vectors))
            return acc + mm(vectors, tile)

        return lax.fori_loop(
            0, nbr.shape[1], slot, jnp.zeros((columns, points), F32), unroll=4
        )

    def sketch_copy(t):
        return remote(
            sketches.at[t],
            z_ref.at[pl.ds(pl.multiple_of(v * columns, columns), columns)],
            sk_send.at[t],
            sk_recv.at[t],
            on_vec((v + 1 + t) % vec_n),
        )

    @pl.loop(0, vec_n - 1)
    def _(t):
        sketches[t] = sketch_of((v + 1 + t) % vec_n)
        sketch_copy(t).start()

    z_ref[pl.ds(pl.multiple_of(v * columns, columns), columns), :] = sketch_of(v)

    @pl.loop(0, vec_n - 1)
    def _(t):
        sketch_copy(t).wait()

    def node(n, z, zt):
        size = zt.shape[0]
        z_parts, zt_parts = split(z), split(zt)
        mean_sq = jnp.sum(z * z) / (size * total) + EPSILON
        gram = split(mm3(zt_parts, z_parts))
        w = (weights[n, 0, :, :size], weights[n, 1, :, :size])
        interp = mm3(w, gram) / (total * mean_sq)
        return interp, mean_sq, zt_parts

    def up_of(interp, mean_sq, zt_parts):
        return mm3(split(interp), zt_parts) * lax.rsqrt(mean_sq)

    map_copies = []
    count = 0

    def send_map(source, out, place, level, count):
        step = 1 << level
        for j in range(1, vec_n >> level):
            map_copies.append(
                remote(
                    source,
                    out.at[place],
                    map_send.at[count],
                    map_recv.at[count],
                    on_vec((v + j * step) % vec_n),
                )
            )
            map_copies[-1].start()
            count += 1
        return count

    own_copies = []

    def own_map(source, target, sem):
        own_copies.append(pltpu.make_async_copy(source, target, sem))
        own_copies[-1].start()

    z = z_ref[...]
    interp, mean_sq, zt_parts = node(0, z, jnp.transpose(z))
    leaf_map[...] = interp
    up = up_of(interp, mean_sq, zt_parts)

    offset = 0
    pending = (leaf_map, out_leaf, v, 0)
    for n in range(1, levels + UPL + 1):
        if n <= levels:
            stride = 1 << (n - 1)
            half = (v // stride) % 2
            if n % 2 == 1:
                partner = on_vec(flip(v, stride))
            else:
                partner = on_vec(flip(flip(v, stride), stride // 2))
        else:
            stride = 1 << (n - levels - 1)
            half = (d // stride) % 2
            partner = on_leaf(upper_partner[n - levels - 1])
        joined[n - 1, half] = up
        exchange = remote(
            joined.at[n - 1, half],
            joined.at[n - 1, half],
            up_send.at[n - 1],
            up_recv.at[n - 1],
            partner,
        )
        exchange.start()
        if pending is not None:
            source, out, place, level = pending
            own_map(source, out.at[place], out_sem.at[n - 1])
            count = send_map(source, out, place, level, count)
        exchange.wait()
        zt = joined[n - 1].reshape(2 * joined.shape[2], total)
        z = jnp.transpose(zt)
        interp, mean_sq, zt_parts = node(n, z, zt)
        node_maps[n - 1] = interp
        if n <= levels:
            pending = (node_maps.at[n - 1], out_local, offset + v // (1 << n), n)
            offset += vec_n >> n
        else:
            pending = None
            own_map(
                node_maps.at[n - 1], out_upper.at[0, n - levels - 1], out_sem.at[n]
            )
        if n < levels + UPL:
            up = up_of(interp, mean_sq, zt_parts)
        else:
            z_top[...] = z
            mine = z_top[pl.ds(pl.multiple_of(v * columns, columns), columns), :]
            out_top[0] = mm3(split(mine), split(interp), NT) * lax.rsqrt(mean_sq)

    for copy in sides:
        copy.wait_send()
    for copy in own_copies:
        copy.wait()
    for copy in map_copies:
        copy.wait()


def on_device(
    leaf_n,
    vec_n,
    axes,
    points,
    probe_vectors,
    neighbours,
    leaf_pivots,
    leaf_inverse,
    local_pivots,
    local_inverse,
    upper_pivots,
    upper_inverse,
):
    group, columns, size = probe_vectors.shape
    rank = leaf_pivots.shape[1]
    slots = neighbours.shape[1]
    levels = vec_n.bit_length() - 1
    total = columns * vec_n
    nodes = levels + UPL
    maps = sum((vec_n >> t) - 1 for t in range(levels))
    vmem = pl.BlockSpec(memory_space=pltpu.VMEM)
    anywhere = pl.BlockSpec(memory_space=pl.ANY)
    smem = pl.BlockSpec(memory_space=pltpu.SMEM)
    dma = pltpu.SemaphoreType.DMA
    leaf_map, local_map, upper_map, top = pl.pallas_call(
        functools.partial(body, leaf_n, vec_n, axes),
        out_shape=(
            jax.ShapeDtypeStruct((group, rank, size), F32),
            jax.ShapeDtypeStruct((group - 1, rank, 2 * rank), F32),
            jax.ShapeDtypeStruct((1, UPL, rank, 2 * rank), F32),
            jax.ShapeDtypeStruct((1, columns, rank), F32),
        ),
        in_specs=[anywhere, anywhere, smem, vmem, anywhere, vmem, anywhere, vmem, anywhere],
        out_specs=(anywhere, anywhere, anywhere, vmem),
        scratch_shapes=[
            pltpu.VMEM((3, 3, group, size), BF16),
            pltpu.VMEM((3 * group, columns, size), BF16),
            pltpu.VMEM((group, 16, size), BF16),
            pltpu.VMEM((3 * group, size, 16), BF16),
            pltpu.VMEM((nodes + 1, rank, rank), F32),
            pltpu.VMEM((nodes + 1, 2, rank, size), BF16),
            pltpu.VMEM((vec_n - 1, columns, size), F32),
            pltpu.VMEM((total, size), F32),
            pltpu.VMEM((nodes, 2, rank, total), F32),
            pltpu.VMEM((total, 2 * rank), F32),
            pltpu.VMEM((rank, size), F32),
            pltpu.VMEM((nodes, rank, 2 * rank), F32),
            dma((nodes + 1,)),
            dma((2,)),
            dma((4,)),
            dma((4,)),
            dma((vec_n - 1,)),
            dma((vec_n - 1,)),
            dma((nodes,)),
            dma((nodes,)),
            dma((maps,)),
            dma((maps,)),
            dma((nodes + 1,)),
        ],
        compiler_params=pltpu.CompilerParams(
            collective_id=0, has_side_effects=True, vmem_limit_bytes=48 * 2**20
        ),
    )(
        jnp.transpose(points, (1, 0, 2)),
        probe_vectors,
        neighbours,
        leaf_pivots,
        leaf_inverse,
        local_pivots,
        local_inverse,
        upper_pivots,
        upper_inverse,
    )
    return (
        jnp.swapaxes(leaf_map, 1, 2),
        jnp.swapaxes(local_map, 1, 2),
        jnp.swapaxes(upper_map, 2, 3),
        top,
    )


def solution(mesh):
    axes = tuple(mesh.axis_names)
    placed = (
        P("leaf", None, None),
        P("leaf", "vec", None),
        P("leaf", None),
        P("leaf", None),
        P("leaf", None, None),
        P("leaf", None),
        P("leaf", None, None),
        P(),
        P(),
    )
    return jax.shard_map(
        functools.partial(on_device, mesh.shape["leaf"], mesh.shape["vec"], axes),
        mesh=mesh,
        in_specs=placed,
        out_specs=(
            P("leaf", None, None),
            P("leaf", None, None),
            P("leaf", None, None, None),
            P("leaf", "vec", None),
        ),
        check_vma=False,
    )
```

```python
import functools

import jax
import jax.numpy as jnp
from jax import lax
from jax.experimental import pallas as pl
from jax.experimental.pallas import tpu as pltpu
from jax.sharding import PartitionSpec as P

UPL = 3
SOFTEN = 0.0009
EPSILON = 1e-06
FLUSH = 4
F32 = jnp.float32
BF16 = jnp.bfloat16
NN = (((1,), (0,)), ((), ()))
NT = (((1,), (1,)), ((), ()))


def mm(a, b, dims=NN):
    return lax.dot_general(a, b, dims, preferred_element_type=F32)


def split(a):
    high = a.astype(BF16)
    return high, (a - high.astype(F32)).astype(BF16)


def mm3(a, b, dims=NN):
    return mm(a[0], b[0], dims) + (mm(a[0], b[1], dims) + mm(a[1], b[0], dims))


def feature_rows(xyz, weight):
    norm = SOFTEN / 2 + xyz[0] * xyz[0] + xyz[1] * xyz[1] + xyz[2] * xyz[2]
    high = norm.astype(BF16).astype(F32)
    rest = norm - high
    middle = rest.astype(BF16).astype(F32)
    low = (rest - middle).astype(BF16).astype(F32)
    return [part * weight for part in (high, middle, low)]


def body(
    leaf_n,
    vec_n,
    axes,
    pts,
    probe,
    nbr_in,
    leaf_piv,
    leaf_inv,
    local_piv,
    local_inv,
    upper_piv,
    upper_inv,
    out_leaf,
    out_local,
    out_upper,
    out_top,
    nbr,
    piv,
    ext_pts,
    ext_probe,
    near,
    far,
    tiles,
    vectors,
    inv,
    weights,
    sketches,
    z_ref,
    joined,
    z_top,
    leaf_map,
    node_maps,
    top_ref,
    inv_sem,
    piv_sem,
    own_sem,
    side_send,
    side_recv,
    sk_send,
    sk_recv,
    up_send,
    up_recv,
    map_send,
    map_recv,
    out_sem,
):
    leaf_axis, vec_axis = axes
    d = lax.axis_index(leaf_axis)
    v = lax.axis_index(vec_axis)
    group, columns, points = probe.shape
    rank = inv.shape[1]
    levels = group.bit_length() - 1
    total = columns * vec_n
    wide = 2 * columns
    slots = nbr.shape[1]
    part = group // 2

    x, y = v % 4, v // 4
    pair, side_row = x // 2, x % 2
    half = ((x + 1) // 2) % 2
    w = part * half + 4 * pair + y

    def vec_of(cluster):
        high, low = cluster // part, (cluster // 4) % 2
        return 4 * (cluster % 4) + 2 * low + (high + low) % 2

    def on_vec(u):
        return {leaf_axis: d, vec_axis: u}

    def on_leaf(g):
        return {leaf_axis: g, vec_axis: v}

    def remote(src, dst, send, recv, target):
        return pltpu.make_async_remote_copy(
            src_ref=src,
            dst_ref=dst,
            send_sem=send,
            recv_sem=recv,
            device_id=target,
            device_id_type=pl.DeviceIdType.MESH,
        )

    def flip(index, stride):
        return index + stride * (1 - 2 * ((index // stride) % 2))

    before = (d + leaf_n - 1) % leaf_n
    after = (d + 1) % leaf_n
    upper_partner = [flip(d, 1 << u) for u in range(UPL)]

    barrier = pltpu.get_barrier_semaphore()
    targets = [on_vec((v + t) % vec_n) for t in range(1, vec_n)]
    targets += [on_leaf(g) for g in [before, after] + upper_partner[1:]]
    for target in targets:
        pl.semaphore_signal(
            barrier, inc=1, device_id=target, device_id_type=pl.DeviceIdType.MESH
        )

    mine = [
        pltpu.make_async_copy(pts, ext_pts.at[1], own_sem.at[0]),
        pltpu.make_async_copy(nbr_in, nbr, own_sem.at[1]),
        pltpu.make_async_copy(
            probe,
            ext_probe.at[
                pl.ds(group, group),
                pl.ds(pl.multiple_of(columns * side_row, columns), columns),
            ],
            own_sem.at[2],
        ),
    ]
    for copy in mine:
        copy.start()
    rows = [(0, leaf_inv, v * 0 + w, w)]
    offset = 0
    for t in range(1, levels + 1):
        place = offset + w // (1 << t)
        rows.append((1, local_inv, place, place))
        offset += group >> t
    offset = 0
    for u in range(1, UPL + 1):
        place = offset + d // (1 << u)
        rows.append((2, upper_inv, place, place))
        offset += leaf_n >> u
    inv_copies = [
        pltpu.make_async_copy(source.at[row], inv.at[n], inv_sem.at[n])
        for n, (_, source, row, _) in enumerate(rows)
    ]
    piv_copies = [
        pltpu.make_async_copy(
            source, piv.at[n, pl.ds(0, source.shape[0])], piv_sem.at[n]
        )
        for n, source in enumerate((leaf_piv, local_piv, upper_piv))
    ]
    for copy in piv_copies + inv_copies:
        copy.start()

    pl.semaphore_wait(barrier, len(targets))

    def strip(place, row):
        return ext_probe.at[
            pl.ds(place * group, group),
            pl.ds(pl.multiple_of(columns * row, columns), columns),
        ]

    ways = [(after, 0), (before, 2)]
    pts_copies = [
        remote(pts, ext_pts.at[place], side_send.at[n], side_recv.at[n], on_leaf(target))
        for n, (target, place) in enumerate(ways)
    ]
    pair_copy = remote(
        probe, strip(1, side_row), side_send.at[2], side_recv.at[2], on_vec(flip(v, 1))
    )
    direct = [
        remote(
            probe,
            strip(place, side_row),
            side_send.at[3 + n],
            side_recv.at[3 + n],
            on_leaf(target),
        )
        for n, (target, place) in enumerate(ways)
    ]
    passed = [
        remote(
            strip(1, 1 - side_row),
            strip(place, 1 - side_row),
            side_send.at[5 + n],
            side_recv.at[5 + n],
            on_leaf(target),
        )
        for n, (target, place) in enumerate(ways)
    ]
    for copy in pts_copies + [pair_copy] + direct:
        copy.start()

    def features(side):
        xyz = [ext_pts[side, c].astype(F32) for c in range(3)]
        norm = feature_rows(xyz, 4096.0)
        one = jnp.ones((1, points), F32)
        pad = jnp.zeros((7, points), F32)
        for r in range(group):
            at = [q[r : r + 1] for q in xyz]
            nm = [q[r : r + 1] for q in norm]
            if side == 1:
                near[r] = jnp.concatenate(at + nm + [one] * 3 + [pad], axis=0).astype(BF16)
            rows_far = [q * -8192.0 for q in at] + [one] * 3 + nm + [pad]
            far[side * group + r] = jnp.transpose(
                jnp.concatenate(rows_far, axis=0)
            ).astype(BF16)

    mine[0].wait()
    features(1)
    pts_copies[0].wait_recv()
    features(0)
    pts_copies[1].wait_recv()
    features(2)
    mine[1].wait()

    first = (d - 1) * group

    def place_of(c, k):
        listed = nbr[c, k]
        return jnp.clip(listed - first, 0, 3 * group - 1), listed >= 0

    def tiles_of(c):
        cluster = half * part + c
        near_c = near[cluster]
        for k in range(slots):
            place, _ = place_of(cluster, k)
            tiles[c, k * points : (k + 1) * points, :] = lax.rsqrt(
                mm(far[place], near_c)
            ).astype(BF16)

    pl.loop(0, 2)(tiles_of)
    mine[2].wait()
    pair_copy.wait_recv()
    for copy in passed:
        copy.start()
    pl.loop(2, part)(tiles_of)

    for copy in piv_copies:
        copy.wait()
    for n, (which, _, _, row) in enumerate(rows):
        inv_copies[n].wait()
        size = points if n == 0 else 2 * rank
        chosen = piv[which, pl.ds(row, 1), :]
        spread = (
            lax.broadcasted_iota(jnp.int32, (size, rank), 0) == chosen
        ).astype(F32).astype(BF16)
        high, low = split(jnp.transpose(inv[n]))
        weights[n, 0, :, :size] = mm(high, spread, NT).astype(BF16)
        weights[n, 1, :, :size] = mm(low, spread, NT).astype(BF16)

    for copy in direct + passed:
        copy.wait_recv()

    z_rows = pl.ds(pl.multiple_of(wide * (2 * y + pair), wide), wide)
    own = w % part

    def sketch_of(c):
        for k in range(slots):
            place, listed = place_of(half * part + c, k)
            block = ext_probe[place]
            vectors[:, k * points : (k + 1) * points] = jnp.where(
                listed, block, jnp.zeros_like(block)
            )
        return mm(vectors[...], tiles[c])

    def sketch_copy(t):
        c = (own + 1 + t) % part
        return c, remote(
            sketches.at[t],
            z_ref.at[z_rows],
            sk_send.at[t],
            sk_recv.at[t],
            on_vec(vec_of(half * part + c)),
        )

    @pl.loop(0, part - 1)
    def _(t):
        c, copy = sketch_copy(t)
        sketches[t] = sketch_of(c)
        copy.start()

    z_ref[z_rows, :] = sketch_of(own)

    @pl.loop(0, part - 1)
    def _(t):
        sketch_copy(t)[1].wait()

    def node(n, z, zt):
        size = zt.shape[0]
        z_parts, zt_parts = split(z), split(zt)
        mean_sq = jnp.sum(z * z) / (size * total) + EPSILON
        gram = split(mm3(zt_parts, z_parts))
        scattered = (weights[n, 0, :, :size], weights[n, 1, :, :size])
        interp = mm3(scattered, gram) / (total * mean_sq)
        return interp, mean_sq, zt_parts

    def up_of(interp, mean_sq, zt_parts):
        return mm3(split(interp), zt_parts) * lax.rsqrt(mean_sq)

    map_copies = []
    own_copies = []

    def send_map(source, out, place, level):
        own_copies.append(
            pltpu.make_async_copy(source, out.at[place], out_sem.at[len(own_copies)])
        )
        own_copies[-1].start()
        step = 1 << level
        for j in range(1, group >> level):
            n = len(map_copies)
            map_copies.append(
                remote(
                    source,
                    out.at[place],
                    map_send.at[n],
                    map_recv.at[n],
                    on_vec(vec_of((w + j * step) % group)),
                )
            )
            map_copies[-1].start()

    z = z_ref[...]
    interp, mean_sq, zt_parts = node(0, z, jnp.transpose(z))
    leaf_map[...] = interp
    up = up_of(interp, mean_sq, zt_parts)

    offset = 0
    pending = [(leaf_map, out_leaf, w, 0)]
    for n in range(1, levels + UPL + 1):
        if n <= levels:
            stride = 1 << (n - 1)
            branch = (w // stride) % 2
            other = flip(w, stride)
            if n == 2:
                other = flip(other, 1)
            partner = on_vec(vec_of(other))
        else:
            stride = 1 << (n - levels - 1)
            branch = (d // stride) % 2
            partner = on_leaf(upper_partner[n - levels - 1])
        joined[n - 1, branch] = up
        exchange = remote(
            joined.at[n - 1, branch],
            joined.at[n - 1, branch],
            up_send.at[n - 1],
            up_recv.at[n - 1],
            partner,
        )
        exchange.start()
        if n >= FLUSH:
            for item in pending:
                send_map(*item)
            pending = []
        exchange.wait()
        zt = joined[n - 1].reshape(2 * rank, total)
        z = jnp.transpose(zt)
        interp, mean_sq, zt_parts = node(n, z, zt)
        node_maps[n - 1] = interp
        if n <= levels:
            pending.append((node_maps.at[n - 1], out_local, offset + w // (1 << n), n))
            offset += group >> n
        else:
            own_copies.append(
                pltpu.make_async_copy(
                    node_maps.at[n - 1],
                    out_upper.at[0, n - levels - 1],
                    out_sem.at[len(own_copies)],
                )
            )
            own_copies[-1].start()
        if n < levels + UPL:
            up = up_of(interp, mean_sq, zt_parts)
        else:
            z_top[...] = z
            kept = z_top[pl.ds(pl.multiple_of(v * columns, columns), columns), :]
            top_ref[0] = mm3(split(kept), split(interp), NT) * lax.rsqrt(mean_sq)
            own_copies.append(
                pltpu.make_async_copy(top_ref, out_top, out_sem.at[len(own_copies)])
            )
            own_copies[-1].start()

    for copy in pts_copies + [pair_copy] + direct + passed:
        copy.wait_send()
    for copy in own_copies:
        copy.wait()
    for copy in map_copies:
        copy.wait()


def write_out(a, b, c, e, out_a, out_b, out_c, out_e, buf_a, buf_b, buf_c, buf_e, in_sem, out_sem):
    pieces = []
    for source, buf, target, step in (
        (a, buf_a, out_a, 4),
        (b, buf_b, out_b, 5),
        (c, buf_c, out_c, 1),
        (e, buf_e, out_e, 1),
    ):
        for start in range(0, source.shape[0], step):
            at = pl.ds(start, step)
            n = len(pieces)
            pieces.append(
                (
                    pltpu.make_async_copy(source.at[at], buf.at[at], in_sem.at[n]),
                    pltpu.make_async_copy(buf.at[at], target.at[at], out_sem.at[n]),
                )
            )
    for arrive, _ in pieces:
        arrive.start()
    for arrive, leave in pieces:
        arrive.wait()
        leave.start()
    for _, leave in pieces:
        leave.wait()


def on_device(
    leaf_n,
    vec_n,
    axes,
    points,
    probe_vectors,
    neighbours,
    leaf_pivots,
    leaf_inverse,
    local_pivots,
    local_inverse,
    upper_pivots,
    upper_inverse,
):
    group, columns, size = probe_vectors.shape
    rank = leaf_pivots.shape[1]
    slots = neighbours.shape[1]
    levels = group.bit_length() - 1
    total = columns * vec_n
    nodes = levels + UPL
    part = group // 2
    pivot_rows = max(p.shape[0] for p in (leaf_pivots, local_pivots, upper_pivots))
    maps = sum((group >> t) - 1 for t in range(levels))
    anywhere = pl.BlockSpec(memory_space=pl.ANY)
    hbm = pl.BlockSpec(memory_space=pltpu.HBM)
    dma = pltpu.SemaphoreType.DMA
    shapes = (
        jax.ShapeDtypeStruct((group, rank, size), F32),
        jax.ShapeDtypeStruct((group - 1, rank, 2 * rank), F32),
        jax.ShapeDtypeStruct((1, UPL, rank, 2 * rank), F32),
        jax.ShapeDtypeStruct((1, columns, rank), F32),
    )
    made = pl.pallas_call(
        functools.partial(body, leaf_n, vec_n, axes),
        out_shape=shapes,
        in_specs=[hbm] * 9,
        out_specs=[anywhere] * 4,
        scratch_shapes=[
            pltpu.SMEM((group, slots), jnp.int32),
            pltpu.VMEM((3, -(-pivot_rows // 8) * 8, rank), jnp.int32),
            pltpu.VMEM((3, 3, group, size), BF16),
            pltpu.VMEM((3 * group, 2 * columns, size), BF16),
            pltpu.VMEM((group, 16, size), BF16),
            pltpu.VMEM((3 * group, size, 16), BF16),
            pltpu.VMEM((part, slots * size, size), BF16),
            pltpu.VMEM((2 * columns, slots * size), BF16),
            pltpu.VMEM((nodes + 1, rank, rank), F32),
            pltpu.VMEM((nodes + 1, 2, rank, size), BF16),
            pltpu.VMEM((part - 1, 2 * columns, size), F32),
            pltpu.VMEM((total, size), F32),
            pltpu.VMEM((nodes, 2, rank, total), F32),
            pltpu.VMEM((total, 2 * rank), F32),
            pltpu.VMEM((rank, size), F32),
            pltpu.VMEM((nodes, rank, 2 * rank), F32),
            pltpu.VMEM((1, columns, rank), F32),
            dma((nodes + 1,)),
            dma((3,)),
            dma((3,)),
            dma((7,)),
            dma((7,)),
            dma((part - 1,)),
            dma((part - 1,)),
            dma((nodes,)),
            dma((nodes,)),
            dma((maps,)),
            dma((maps,)),
            dma((nodes + 2,)),
        ],
        compiler_params=pltpu.CompilerParams(
            collective_id=0, has_side_effects=True, vmem_limit_bytes=60 * 2**20
        ),
    )(
        jnp.transpose(points, (1, 0, 2)),
        probe_vectors,
        neighbours,
        leaf_pivots,
        leaf_inverse,
        local_pivots,
        local_inverse,
        upper_pivots,
        upper_inverse,
    )
    leaf_map, local_map, upper_map, top = pl.pallas_call(
        write_out,
        out_shape=shapes,
        in_specs=[anywhere] * 4,
        out_specs=[hbm] * 4,
        scratch_shapes=[pltpu.VMEM(p.shape, p.dtype) for p in shapes] + [dma((9,))] * 2,
        compiler_params=pltpu.CompilerParams(vmem_limit_bytes=60 * 2**20),
    )(*made)
    return (
        jnp.swapaxes(leaf_map, 1, 2),
        jnp.swapaxes(local_map, 1, 2),
        jnp.swapaxes(upper_map, 2, 3),
        top,
    )


def solution(mesh):
    axes = tuple(mesh.axis_names)
    placed = (
        P("leaf", None, None),
        P("leaf", "vec", None),
        P("leaf", None),
        P("leaf", None),
        P("leaf", None, None),
        P("leaf", None),
        P("leaf", None, None),
        P(),
        P(),
    )
    return jax.shard_map(
        functools.partial(on_device, mesh.shape["leaf"], mesh.shape["vec"], axes),
        mesh=mesh,
        in_specs=placed,
        out_specs=(
            P("leaf", None, None),
            P("leaf", None, None),
            P("leaf", None, None, None),
            P("leaf", "vec", None),
        ),
        check_vma=False,
    )
```

```python
import functools

import jax
import jax.numpy as jnp
from jax import lax
from jax.experimental import pallas as pl
from jax.experimental.pallas import tpu as pltpu
from jax.sharding import PartitionSpec as P

UPL = 3
SOFTEN = 0.0009
EPSILON = 1e-06
F32 = jnp.float32
BF16 = jnp.bfloat16
NN = (((1,), (0,)), ((), ()))
NT = (((1,), (1,)), ((), ()))


def mm(a, b, dims=NN):
    return lax.dot_general(a, b, dims, preferred_element_type=F32)


def split(a):
    high = a.astype(BF16)
    return high, (a - high.astype(F32)).astype(BF16)


def mm3(a, b, dims=NN):
    return mm(a[0], b[0], dims) + (mm(a[0], b[1], dims) + mm(a[1], b[0], dims))


def feature_rows(xyz, weight):
    norm = SOFTEN / 2 + xyz[0] * xyz[0] + xyz[1] * xyz[1] + xyz[2] * xyz[2]
    high = norm.astype(BF16).astype(F32)
    rest = norm - high
    middle = rest.astype(BF16).astype(F32)
    low = (rest - middle).astype(BF16).astype(F32)
    return [part * weight for part in (high, middle, low)]


def body(
    leaf_n,
    vec_n,
    axes,
    pts,
    probe,
    nbr_in,
    leaf_piv,
    leaf_inv,
    local_piv,
    local_inv,
    upper_piv,
    upper_inv,
    out_leaf,
    out_local,
    out_upper,
    out_top,
    nbr,
    piv,
    ext_pts,
    ext_probe,
    near,
    far,
    tiles,
    vectors,
    inv,
    weights,
    upper_weights,
    sketches,
    z_ref,
    quad,
    twin,
    joined,
    z_top,
    leaf_map,
    maps,
    upper_maps,
    top_ref,
    inv_sem,
    piv_sem,
    own_sem,
    side_send,
    side_recv,
    sk_send,
    sk_recv,
    ex_send,
    ex_recv,
    mate_send,
    mate_recv,
    map_send,
    map_recv,
    out_sem,
):
    leaf_axis, vec_axis = axes
    d = lax.axis_index(leaf_axis)
    v = lax.axis_index(vec_axis)
    group, columns, points = probe.shape
    rank = inv.shape[1]
    total = columns * vec_n
    wide = 2 * columns
    slots = nbr.shape[1]
    part = group // 2

    x, y = v % 4, v // 4
    pair, side_row = x // 2, x % 2
    half = ((x + 1) // 2) % 2
    w = part * half + 4 * pair + y
    own = w % part
    core = d % 2
    lead = core == 1

    def vec_of(cluster):
        high, low = cluster // part, (cluster // 4) % 2
        return 4 * (cluster % 4) + 2 * low + (high + low) % 2

    def on_vec(u):
        return {leaf_axis: d, vec_axis: u}

    def on_leaf(g):
        return {leaf_axis: g, vec_axis: v}

    def remote(src, dst, send, recv, target):
        return pltpu.make_async_remote_copy(
            src_ref=src,
            dst_ref=dst,
            send_sem=send,
            recv_sem=recv,
            device_id=target,
            device_id_type=pl.DeviceIdType.MESH,
        )

    def flip(index, stride):
        return index + stride * (1 - 2 * ((index // stride) % 2))

    before = (d + leaf_n - 1) % leaf_n
    after = (d + 1) % leaf_n
    mate = flip(d, 1)
    lead_row = d - core + 1

    barrier = pltpu.get_barrier_semaphore()
    targets = [on_vec((v + t) % vec_n) for t in range(1, vec_n)]
    targets += [on_leaf(g) for g in (before, after, flip(d, 2), flip(d, 4))]
    targets += [
        {leaf_axis: mate, vec_axis: vec_of(half * part + (own + t) % part)}
        for t in range(1, part)
    ]
    for target in targets:
        pl.semaphore_signal(
            barrier, inc=1, device_id=target, device_id_type=pl.DeviceIdType.MESH
        )

    mine = [
        pltpu.make_async_copy(pts, ext_pts.at[1], own_sem.at[0]),
        pltpu.make_async_copy(nbr_in, nbr, own_sem.at[1]),
        pltpu.make_async_copy(
            probe,
            ext_probe.at[
                pl.ds(group, group),
                pl.ds(pl.multiple_of(columns * side_row, columns), columns),
            ],
            own_sem.at[2],
        ),
    ]
    quarter = w // 4
    rows = [(0, leaf_inv, w)]
    rows += [(1, local_inv, 2 * quarter + n) for n in range(2)]
    rows += [(1, local_inv, group // 2 + quarter)]
    rows += [(1, local_inv, group - 4 + n) for n in range(3)]
    local_nodes = len(rows)
    offset = 0
    for u in range(1, UPL + 1):
        rows.append((2, upper_inv, offset + d // (1 << u)))
        offset += leaf_n >> u
    inv_copies = [
        pltpu.make_async_copy(source.at[row], inv.at[n], inv_sem.at[n])
        for n, (_, source, row) in enumerate(rows)
    ]
    piv_copies = [
        pltpu.make_async_copy(
            source, piv.at[n, pl.ds(0, source.shape[0])], piv_sem.at[n]
        )
        for n, source in enumerate((leaf_piv, local_piv, upper_piv))
    ]
    for copy in mine[:1] + piv_copies + inv_copies + mine[1:]:
        copy.start()

    def features(side):
        xyz = [ext_pts[side, c].astype(F32) for c in range(3)]
        norm = feature_rows(xyz, 4096.0)
        one = jnp.ones((1, points), F32)
        pad = jnp.zeros((7, points), F32)
        for r in range(group):
            at = [q[r : r + 1] for q in xyz]
            nm = [q[r : r + 1] for q in norm]
            if side == 1:
                near[r] = jnp.concatenate(at + nm + [one] * 3 + [pad], axis=0).astype(BF16)
            rows_far = [q * -8192.0 for q in at] + [one] * 3 + nm + [pad]
            far[side * group + r] = jnp.transpose(
                jnp.concatenate(rows_far, axis=0)
            ).astype(BF16)

    mine[0].wait()
    features(1)

    for copy in piv_copies:
        copy.wait()
    for n, (which, _, row) in enumerate(rows):
        inv_copies[n].wait()
        size = points if n == 0 else 2 * rank
        chosen = piv[which, pl.ds(row, 1), :]
        spread = (
            lax.broadcasted_iota(jnp.int32, (size, rank), 0) == chosen
        ).astype(F32).astype(BF16)
        for m, piece in enumerate(split(jnp.transpose(inv[n]))):
            scattered = mm(piece, spread, NT).astype(BF16)
            if n < local_nodes:
                weights[core, n, m, :, :size] = scattered
            else:
                upper_weights[n - local_nodes, m] = scattered
    mine[1].wait()
    mine[2].wait()

    pl.semaphore_wait(barrier, len(targets))

    def strip(place, row, piece=None):
        start, count = place * group, group
        if piece is not None:
            start, count = start + piece * part, part
        return ext_probe.at[
            pl.ds(start, count), pl.ds(pl.multiple_of(columns * row, columns), columns)
        ]

    ways = [(after, 0), (before, 2)]
    pts_copies = [
        remote(pts, ext_pts.at[place], side_send.at[n], side_recv.at[n], on_leaf(target))
        for n, (target, place) in enumerate(ways)
    ]
    pair_copies = [
        remote(
            probe.at[pl.ds(piece * part, part)],
            strip(1, side_row, piece),
            side_send.at[2 + piece],
            side_recv.at[2 + piece],
            on_vec(flip(v, 1)),
        )
        for piece in range(2)
    ]
    direct = [
        remote(
            probe,
            strip(place, side_row),
            side_send.at[4 + n],
            side_recv.at[4 + n],
            on_leaf(target),
        )
        for n, (target, place) in enumerate(ways)
    ]

    def passed(piece):
        return [
            remote(
                strip(1, 1 - side_row, piece),
                strip(place, 1 - side_row, piece),
                side_send.at[6 + 2 * piece + n],
                side_recv.at[6 + 2 * piece + n],
                on_leaf(target),
            )
            for n, (target, place) in enumerate(ways)
        ]

    for copy in pts_copies + pair_copies + direct:
        copy.start()

    def hand(n, src, dst):
        return remote(src, dst, mate_send.at[n], mate_recv.at[n], on_leaf(mate))

    give_weights = hand(0, weights.at[0], weights.at[0])

    @pl.when(core == 0)
    def _():
        give_weights.start()

    pts_copies[0].wait_recv()
    features(0)
    pts_copies[1].wait_recv()
    features(2)

    first = (d - 1) * group

    def place_of(c, k):
        listed = nbr[c, k]
        return jnp.clip(listed - first, 0, 3 * group - 1), listed >= 0

    @pl.loop(0, part)
    def _(c):
        cluster = half * part + c
        near_c = near[cluster]
        for k in range(slots):
            place, _ = place_of(cluster, k)
            tiles[c, k * points : (k + 1) * points, :] = lax.rsqrt(
                mm(far[place], near_c)
            ).astype(BF16)
        for piece in range(2):

            @pl.when(c == 2 * piece)
            def _():
                pair_copies[piece].wait_recv()
                for copy in passed(piece):
                    copy.start()

    for copy in direct + passed(0) + passed(1):
        copy.wait_recv()

    z_rows = pl.ds(pl.multiple_of(wide * (2 * y + pair), wide), wide)

    def sketch_copy(t, origin):
        c = half * part + (own + 1 + t) % part
        return remote(
            sketches.at[t],
            z_ref.at[origin, z_rows],
            sk_send.at[t],
            sk_recv.at[origin, t],
            {leaf_axis: lead_row, vec_axis: vec_of(c)},
        )

    last = hand(1, sketches.at[part - 1], z_ref.at[0, z_rows])

    @pl.loop(0, part)
    def _(t):
        c = (own + 1 + t) % part
        for k in range(slots):
            place, listed = place_of(half * part + c, k)
            block = ext_probe[place]
            vectors[:, k * points : (k + 1) * points] = jnp.where(
                listed, block, jnp.zeros_like(block)
            )
        sketches[t] = mm(vectors[...], tiles[c])

        @pl.when(t < part - 1)
        def _():
            sketch_copy(t, core).start()

    place_a = pl.ds(2 * quarter, 2)

    def publish_leaf():
        copies = [pltpu.make_async_copy(leaf_map.at[core], out_leaf.at[w], out_sem.at[0])]
        for j in range(1, group):
            copies.append(
                remote(
                    leaf_map.at[core],
                    out_leaf.at[w],
                    map_send.at[j - 1],
                    map_recv.at[j - 1],
                    on_vec(vec_of((w + j) % group)),
                )
            )
        return copies

    def publish_local():
        blocks = [
            (maps.at[core, pl.ds(0, 2)], out_local.at[place_a]),
            (maps.at[core, 2], out_local.at[group // 2 + quarter]),
        ]
        copies = [
            pltpu.make_async_copy(src, dst, out_sem.at[1 + n])
            for n, (src, dst) in enumerate(blocks)
        ]
        for j in range(1, 4):
            target = on_vec(vec_of((w + 4 * j) % group))
            for n, (src, dst) in enumerate(blocks):
                m = group - 1 + 2 * (j - 1) + n
                copies.append(remote(src, dst, map_send.at[m], map_recv.at[m], target))
        return copies

    give_leaf = hand(2, leaf_map.at[0], leaf_map.at[0])
    give_a = hand(3, maps.at[0, pl.ds(0, 3)], maps.at[0, pl.ds(0, 3)])
    top_rows = pl.ds(group - 4, 3)
    give_b = hand(4, maps.at[0, pl.ds(3, 3)], out_local.at[top_rows])
    give_upper = [
        hand(5 + u, upper_maps.at[u], out_upper.at[0, u]) for u in range(UPL)
    ]
    give_top = hand(5 + UPL, top_ref, out_top)
    gifts = [give_b] + give_upper + [give_top]

    def peer(r, k):
        pos = w % 4 if r == 0 else quarter
        other = flip(pos, k) if k < 3 else 3 - pos
        cluster = 4 * quarter + other if r == 0 else 4 * other + w % 4
        return pos, on_vec(vec_of(cluster))

    def round_copy(r, k):
        pos, target = peer(r, k)
        return remote(
            quad.at[r, pos],
            quad.at[r, pos],
            ex_send.at[3 * r + k - 1],
            ex_recv.at[3 * r + k - 1],
            target,
        )

    def upper_copy(u):
        branch = (d // (1 << u)) % 2
        return remote(
            joined.at[u - 1, branch],
            joined.at[u - 1, branch],
            ex_send.at[5 + u],
            ex_recv.at[5 + u],
            on_leaf(flip(d, 1 << u)),
        )

    def node(scattered, z, zt):
        size = zt.shape[0]
        z_parts, zt_parts = split(z), split(zt)
        mean_sq = jnp.sum(z * z) / (size * total) + EPSILON
        gram = split(mm3(zt_parts, z_parts))
        interp = mm3(scattered, gram) / (total * mean_sq)
        return interp, mean_sq, zt_parts

    def up_of(interp, mean_sq, zt_parts):
        return mm3(split(interp), zt_parts) * lax.rsqrt(mean_sq)

    def join(left, right):
        zt = jnp.concatenate([left, right], axis=0)
        return jnp.transpose(zt), zt

    def local_weights(g, n):
        return weights[g, n, 0, :, : 2 * rank], weights[g, n, 1, :, : 2 * rank]

    @pl.when(core == 0)
    def _():
        last.start()
        give_leaf.wait_recv()
        for copy in publish_leaf():
            copy.start()
        give_a.wait_recv()
        for copy in publish_local():
            copy.start()
        for copy in gifts:
            copy.wait_recv()
        give_weights.wait_send()
        last.wait_send()

    @pl.when(lead)
    def _():
        z_ref[1, z_rows, :] = sketches[part - 1]
        give_weights.wait_recv()

        @pl.loop(0, part - 1)
        def _(t):
            sketch_copy(t, 1).wait_recv()
            sketch_copy(t, 0).wait_recv()

        last.wait_recv()
        pos = w % 4
        for g in range(2):
            z = z_ref[g]
            made = node((weights[g, 0, 0], weights[g, 0, 1]), z, jnp.transpose(z))
            leaf_map[g] = made[0]
            quad[0, pos, g] = up_of(*made)
        for r in range(2):
            pos = w % 4 if r == 0 else quarter
            branch = pos // 2
            for k in (1, 3, 2):
                round_copy(r, k).start()
            if r == 1:
                give_leaf.start()
                give_a.start()
                for copy in publish_leaf() + publish_local():
                    copy.start()
            for which, side in ((0, branch), (1, 1 - branch)):
                for k in ((1,), (2, 3))[which]:
                    round_copy(r, k).wait_recv()
                for g in range(2):
                    z, zt = join(quad[r, 2 * side, g], quad[r, 2 * side + 1, g])
                    made = node(local_weights(g, 1 + 3 * r + side), z, zt)
                    maps[g, 3 * r + side] = made[0]
                    twin[r, side, g] = up_of(*made)
            for g in range(2):
                z, zt = join(twin[r, 0, g], twin[r, 1, g])
                made = node(local_weights(g, 3 + 3 * r), z, zt)
                maps[g, 3 * r + 2] = made[0]
                if r == 0:
                    quad[1, quarter, g] = up_of(*made)
                else:
                    twin[2, 0, g] = up_of(*made)
        give_b.start()
        own_b = pltpu.make_async_copy(
            maps.at[1, pl.ds(3, 3)], out_local.at[top_rows], out_sem.at[3]
        )
        own_b.start()
        z, zt = join(twin[2, 0, 0], twin[2, 0, 1])
        own_upper = []
        for u in range(UPL):
            made = node((upper_weights[u, 0], upper_weights[u, 1]), z, zt)
            upper_maps[u] = made[0]
            if u + 1 < UPL:
                joined[u, (d // (2 << u)) % 2] = up_of(*made)
                upper_copy(u + 1).start()
            give_upper[u].start()
            own_upper.append(
                pltpu.make_async_copy(
                    upper_maps.at[u], out_upper.at[0, u], out_sem.at[4 + u]
                )
            )
            own_upper[-1].start()
            if u + 1 < UPL:
                upper_copy(u + 1).wait_recv()
                z, zt = join(joined[u, 0], joined[u, 1])
            else:
                z_top[...] = z
                kept = z_top[pl.ds(pl.multiple_of(v * columns, columns), columns), :]
                top_ref[0] = mm3(split(kept), split(made[0]), NT) * lax.rsqrt(made[1])
        give_top.start()
        own_top = pltpu.make_async_copy(top_ref, out_top, out_sem.at[4 + UPL])
        own_top.start()
        for copy in [own_b, own_top] + own_upper:
            copy.wait()
        for copy in [give_leaf, give_a] + gifts:
            copy.wait_send()
        for r in range(2):
            for k in range(1, 4):
                round_copy(r, k).wait_send()
        for u in range(1, UPL):
            upper_copy(u).wait_send()

    @pl.loop(0, part - 1)
    def _(t):
        sketch_copy(t, core).wait_send()

    for copy in pts_copies + pair_copies + direct + passed(0) + passed(1):
        copy.wait_send()
    for copy in publish_leaf() + publish_local():
        copy.wait()


def write_out(a, b, c, e, out_a, out_b, out_c, out_e, buf_a, buf_b, buf_c, buf_e, in_sem, out_sem):
    pieces = []
    for source, buf, target, step in (
        (a, buf_a, out_a, 4),
        (b, buf_b, out_b, 5),
        (c, buf_c, out_c, 1),
        (e, buf_e, out_e, 1),
    ):
        for start in range(0, source.shape[0], step):
            at = pl.ds(start, step)
            n = len(pieces)
            pieces.append(
                (
                    pltpu.make_async_copy(source.at[at], buf.at[at], in_sem.at[n]),
                    pltpu.make_async_copy(buf.at[at], target.at[at], out_sem.at[n]),
                )
            )
    for arrive, _ in pieces:
        arrive.start()
    for arrive, leave in pieces:
        arrive.wait()
        leave.start()
    for _, leave in pieces:
        leave.wait()


def on_device(
    leaf_n,
    vec_n,
    axes,
    points,
    probe_vectors,
    neighbours,
    leaf_pivots,
    leaf_inverse,
    local_pivots,
    local_inverse,
    upper_pivots,
    upper_inverse,
):
    group, columns, size = probe_vectors.shape
    rank = leaf_pivots.shape[1]
    slots = neighbours.shape[1]
    total = columns * vec_n
    part = group // 2
    pivot_rows = max(p.shape[0] for p in (leaf_pivots, local_pivots, upper_pivots))
    anywhere = pl.BlockSpec(memory_space=pl.ANY)
    hbm = pl.BlockSpec(memory_space=pltpu.HBM)
    dma = pltpu.SemaphoreType.DMA
    shapes = (
        jax.ShapeDtypeStruct((group, rank, size), F32),
        jax.ShapeDtypeStruct((group - 1, rank, 2 * rank), F32),
        jax.ShapeDtypeStruct((1, UPL, rank, 2 * rank), F32),
        jax.ShapeDtypeStruct((1, columns, rank), F32),
    )
    made = pl.pallas_call(
        functools.partial(body, leaf_n, vec_n, axes),
        out_shape=shapes,
        in_specs=[hbm] * 9,
        out_specs=[anywhere] * 4,
        scratch_shapes=[
            pltpu.SMEM((group, slots), jnp.int32),
            pltpu.VMEM((3, -(-pivot_rows // 8) * 8, rank), jnp.int32),
            pltpu.VMEM((3, 3, group, size), BF16),
            pltpu.VMEM((3 * group, 2 * columns, size), BF16),
            pltpu.VMEM((group, 16, size), BF16),
            pltpu.VMEM((3 * group, size, 16), BF16),
            pltpu.VMEM((part, slots * size, size), BF16),
            pltpu.VMEM((2 * columns, slots * size), BF16),
            pltpu.VMEM((7 + UPL, rank, rank), F32),
            pltpu.VMEM((2, 7, 2, rank, size), BF16),
            pltpu.VMEM((UPL, 2, rank, 2 * rank), BF16),
            pltpu.VMEM((part, 2 * columns, size), F32),
            pltpu.VMEM((2, total, size), F32),
            pltpu.VMEM((2, 4, 2, rank, total), F32),
            pltpu.VMEM((3, 2, 2, rank, total), F32),
            pltpu.VMEM((UPL - 1, 2, rank, total), F32),
            pltpu.VMEM((total, 2 * rank), F32),
            pltpu.VMEM((2, rank, size), F32),
            pltpu.VMEM((2, 6, rank, 2 * rank), F32),
            pltpu.VMEM((UPL, rank, 2 * rank), F32),
            pltpu.VMEM((1, columns, rank), F32),
            dma((7 + UPL,)),
            dma((3,)),
            dma((3,)),
            dma((10,)),
            dma((10,)),
            dma((part,)),
            dma((2, part)),
            dma((6 + UPL,)),
            dma((6 + UPL,)),
            dma((6 + UPL,)),
            dma((6 + UPL,)),
            dma((group + 5,)),
            dma((group + 5,)),
            dma((5 + UPL,)),
        ],
        compiler_params=pltpu.CompilerParams(
            collective_id=0, has_side_effects=True, vmem_limit_bytes=60 * 2**20
        ),
    )(
        jnp.transpose(points, (1, 0, 2)),
        probe_vectors,
        neighbours,
        leaf_pivots,
        leaf_inverse,
        local_pivots,
        local_inverse,
        upper_pivots,
        upper_inverse,
    )
    leaf_map, local_map, upper_map, top = pl.pallas_call(
        write_out,
        out_shape=shapes,
        in_specs=[anywhere] * 4,
        out_specs=[hbm] * 4,
        scratch_shapes=[pltpu.VMEM(p.shape, p.dtype) for p in shapes] + [dma((9,))] * 2,
        compiler_params=pltpu.CompilerParams(vmem_limit_bytes=60 * 2**20),
    )(*made)
    return (
        jnp.swapaxes(leaf_map, 1, 2),
        jnp.swapaxes(local_map, 1, 2),
        jnp.swapaxes(upper_map, 2, 3),
        top,
    )


def solution(mesh):
    axes = tuple(mesh.axis_names)
    placed = (
        P("leaf", None, None),
        P("leaf", "vec", None),
        P("leaf", None),
        P("leaf", None),
        P("leaf", None, None),
        P("leaf", None),
        P("leaf", None, None),
        P(),
        P(),
    )
    return jax.shard_map(
        functools.partial(on_device, mesh.shape["leaf"], mesh.shape["vec"], axes),
        mesh=mesh,
        in_specs=placed,
        out_specs=(
            P("leaf", None, None),
            P("leaf", None, None),
            P("leaf", None, None, None),
            P("leaf", "vec", None),
        ),
        check_vma=False,
    )
```

```python
import functools

import jax
import jax.numpy as jnp
from jax import lax
from jax.experimental import pallas as pl
from jax.experimental.pallas import tpu as pltpu
from jax.sharding import PartitionSpec as P

UPL = 3
SOFTEN = 0.0009
EPSILON = 1e-06
F32 = jnp.float32
BF16 = jnp.bfloat16
NN = (((1,), (0,)), ((), ()))
NT = (((1,), (1,)), ((), ()))


def mm(a, b, dims=NN):
    return lax.dot_general(a, b, dims, preferred_element_type=F32)


def split(a):
    high = a.astype(BF16)
    return high, (a - high.astype(F32)).astype(BF16)


def mm3(a, b, dims=NN):
    return mm(a[0], b[0], dims) + (mm(a[0], b[1], dims) + mm(a[1], b[0], dims))


def feature_rows(xyz, weight):
    norm = SOFTEN / 2 + xyz[0] * xyz[0] + xyz[1] * xyz[1] + xyz[2] * xyz[2]
    high = norm.astype(BF16).astype(F32)
    rest = norm - high
    middle = rest.astype(BF16).astype(F32)
    low = (rest - middle).astype(BF16).astype(F32)
    return [part * weight for part in (high, middle, low)]


def body(
    leaf_n,
    vec_n,
    axes,
    pts,
    probe,
    nbr_in,
    leaf_piv,
    leaf_inv,
    local_piv,
    local_inv,
    upper_piv,
    upper_inv,
    out_leaf,
    out_local,
    out_upper,
    out_top,
    nbr,
    piv,
    ext_pts,
    ext_probe,
    near,
    far,
    tiles,
    vectors,
    inv,
    weights,
    upper_weights,
    sketches,
    z_ref,
    quad,
    twin,
    joined,
    z_top,
    leaf_map,
    all_leaf,
    all_local,
    maps,
    upper_maps,
    top_ref,
    inv_sem,
    piv_sem,
    own_sem,
    side_send,
    side_recv,
    sk_send,
    sk_recv,
    ex_send,
    ex_recv,
    mate_send,
    mate_recv,
    map_send,
    map_recv,
    out_sem,
):
    leaf_axis, vec_axis = axes
    d = lax.axis_index(leaf_axis)
    v = lax.axis_index(vec_axis)
    group, columns, points = probe.shape
    rank = inv.shape[1]
    total = columns * vec_n
    wide = 2 * columns
    slots = nbr.shape[1]
    part = group // 2

    x, y = v % 4, v // 4
    pair, side_row = x // 2, x % 2
    half = ((x + 1) // 2) % 2
    w = part * half + 4 * pair + y
    own = w % part
    core = d % 2
    lead = core == 1

    def vec_of(cluster):
        high, low = cluster // part, (cluster // 4) % 2
        return 4 * (cluster % 4) + 2 * low + (high + low) % 2

    def on_vec(u):
        return {leaf_axis: d, vec_axis: u}

    def on_leaf(g):
        return {leaf_axis: g, vec_axis: v}

    def remote(src, dst, send, recv, target):
        return pltpu.make_async_remote_copy(
            src_ref=src,
            dst_ref=dst,
            send_sem=send,
            recv_sem=recv,
            device_id=target,
            device_id_type=pl.DeviceIdType.MESH,
        )

    def flip(index, stride):
        return index + stride * (1 - 2 * ((index // stride) % 2))

    before = (d + leaf_n - 1) % leaf_n
    after = (d + 1) % leaf_n
    mate = flip(d, 1)
    lead_row = d - core + 1

    barrier = pltpu.get_barrier_semaphore()
    targets = [on_vec((v + t) % vec_n) for t in range(1, vec_n)]
    targets += [on_leaf(g) for g in (before, after, flip(d, 2), flip(d, 4))]
    targets += [
        {leaf_axis: mate, vec_axis: vec_of(half * part + (own + t) % part)}
        for t in range(1, part)
    ]
    for target in targets:
        pl.semaphore_signal(
            barrier, inc=1, device_id=target, device_id_type=pl.DeviceIdType.MESH
        )

    mine = [
        pltpu.make_async_copy(pts, ext_pts.at[1], own_sem.at[0]),
        pltpu.make_async_copy(nbr_in, nbr, own_sem.at[1]),
        pltpu.make_async_copy(
            probe,
            ext_probe.at[
                pl.ds(group, group),
                pl.ds(pl.multiple_of(columns * side_row, columns), columns),
            ],
            own_sem.at[2],
        ),
    ]
    quarter = w // 4
    rows = [(0, leaf_inv, w)]
    rows += [(1, local_inv, 2 * quarter + n) for n in range(2)]
    rows += [(1, local_inv, group // 2 + quarter)]
    rows += [(1, local_inv, group - 4 + n) for n in range(3)]
    local_nodes = len(rows)
    offset = 0
    for u in range(1, UPL + 1):
        rows.append((2, upper_inv, offset + d // (1 << u)))
        offset += leaf_n >> u
    inv_copies = [
        pltpu.make_async_copy(source.at[row], inv.at[n], inv_sem.at[n])
        for n, (_, source, row) in enumerate(rows)
    ]
    piv_copies = [
        pltpu.make_async_copy(
            source, piv.at[n, pl.ds(0, source.shape[0])], piv_sem.at[n]
        )
        for n, source in enumerate((leaf_piv, local_piv, upper_piv))
    ]
    for copy in mine[:1] + piv_copies + inv_copies + mine[1:]:
        copy.start()

    def features(side):
        xyz = [ext_pts[side, c].astype(F32) for c in range(3)]
        norm = feature_rows(xyz, 4096.0)
        one = jnp.ones((1, points), F32)
        pad = jnp.zeros((7, points), F32)
        for r in range(group):
            at = [q[r : r + 1] for q in xyz]
            nm = [q[r : r + 1] for q in norm]
            if side == 1:
                near[r] = jnp.concatenate(at + nm + [one] * 3 + [pad], axis=0).astype(BF16)
            rows_far = [q * -8192.0 for q in at] + [one] * 3 + nm + [pad]
            far[side * group + r] = jnp.transpose(
                jnp.concatenate(rows_far, axis=0)
            ).astype(BF16)

    mine[0].wait()
    features(1)

    for copy in piv_copies:
        copy.wait()
    for n, (which, _, row) in enumerate(rows):
        inv_copies[n].wait()
        size = points if n == 0 else 2 * rank
        chosen = piv[which, pl.ds(row, 1), :]
        spread = (
            lax.broadcasted_iota(jnp.int32, (size, rank), 0) == chosen
        ).astype(F32).astype(BF16)
        for m, piece in enumerate(split(jnp.transpose(inv[n]))):
            scattered = mm(piece, spread, NT).astype(BF16)
            if n < local_nodes:
                weights[core, n, m, :, :size] = scattered
            else:
                upper_weights[n - local_nodes, m] = scattered
    mine[1].wait()
    mine[2].wait()

    pl.semaphore_wait(barrier, len(targets))

    def strip(place, row, piece=None):
        start, count = place * group, group
        if piece is not None:
            start, count = start + piece * part, part
        return ext_probe.at[
            pl.ds(start, count), pl.ds(pl.multiple_of(columns * row, columns), columns)
        ]

    ways = [(after, 0), (before, 2)]
    pts_copies = [
        remote(pts, ext_pts.at[place], side_send.at[n], side_recv.at[n], on_leaf(target))
        for n, (target, place) in enumerate(ways)
    ]
    pair_copies = [
        remote(
            probe.at[pl.ds(piece * part, part)],
            strip(1, side_row, piece),
            side_send.at[2 + piece],
            side_recv.at[2 + piece],
            on_vec(flip(v, 1)),
        )
        for piece in range(2)
    ]
    direct = [
        remote(
            probe,
            strip(place, side_row),
            side_send.at[4 + n],
            side_recv.at[4 + n],
            on_leaf(target),
        )
        for n, (target, place) in enumerate(ways)
    ]

    def passed(piece):
        return [
            remote(
                strip(1, 1 - side_row, piece),
                strip(place, 1 - side_row, piece),
                side_send.at[6 + 2 * piece + n],
                side_recv.at[6 + 2 * piece + n],
                on_leaf(target),
            )
            for n, (target, place) in enumerate(ways)
        ]

    for copy in pts_copies + pair_copies + direct:
        copy.start()

    def hand(n, src, dst):
        return remote(src, dst, mate_send.at[n], mate_recv.at[n], on_leaf(mate))

    give_weights = hand(0, weights.at[0], weights.at[0])

    @pl.when(core == 0)
    def _():
        give_weights.start()

    pts_copies[0].wait_recv()
    features(0)
    pts_copies[1].wait_recv()
    features(2)

    first = (d - 1) * group

    def place_of(c, k):
        listed = nbr[c, k]
        return jnp.clip(listed - first, 0, 3 * group - 1), listed >= 0

    @pl.loop(0, part)
    def _(c):
        cluster = half * part + c
        near_c = near[cluster]
        for k in range(slots):
            place, _ = place_of(cluster, k)
            tiles[c, k * points : (k + 1) * points, :] = lax.rsqrt(
                mm(far[place], near_c)
            ).astype(BF16)
        for piece in range(2):

            @pl.when(c == 2 * piece)
            def _():
                pair_copies[piece].wait_recv()
                for copy in passed(piece):
                    copy.start()

    for copy in direct + passed(0) + passed(1):
        copy.wait_recv()

    z_rows = pl.ds(pl.multiple_of(wide * (2 * y + pair), wide), wide)

    def sketch_copy(t, origin):
        c = half * part + (own + 1 + t) % part
        return remote(
            sketches.at[t],
            z_ref.at[origin, z_rows],
            sk_send.at[t],
            sk_recv.at[origin, t],
            {leaf_axis: lead_row, vec_axis: vec_of(c)},
        )

    last = hand(1, sketches.at[part - 1], z_ref.at[0, z_rows])

    @pl.loop(0, part)
    def _(t):
        c = (own + 1 + t) % part
        for k in range(slots):
            place, listed = place_of(half * part + c, k)
            block = ext_probe[place]
            vectors[:, k * points : (k + 1) * points] = jnp.where(
                listed, block, jnp.zeros_like(block)
            )
        sketches[t] = mm(vectors[...], tiles[c])

        @pl.when(t < part - 1)
        def _():
            sketch_copy(t, core).start()

    def column(q):
        return 2 * (((q + 1) // 2) % 2) + q // 2

    def along(sem, src, dst, step_x, step_y):
        return remote(
            src,
            dst,
            map_send.at[sem],
            map_recv.at[sem],
            on_vec(4 * ((y + step_y) % 4) + (x + step_x) % 4),
        )

    def same(sem, ref, step_x, step_y):
        return along(sem, ref, ref, step_x, step_y)

    steps = (1, 3)
    order = (0, 3, 1, 2)

    def full_x(way, o):
        return same(
            4 * way + o, all_leaf.at[x, :, (y + order[o]) % 4], steps[way], 0
        )

    def half_x(way, o):
        source = (x + 4 - steps[way]) % 4
        return same(
            8 + 4 * way + o,
            all_leaf.at[source, way, (y + order[o]) % 4],
            steps[way],
            0,
        )

    def full_y(way):
        return same(16 + way, all_leaf.at[x, :, y], 0, steps[way])

    def half_y(way):
        source = (y + 4 - steps[way]) % 4
        return same(18 + way, all_leaf.at[x, way, source], 0, steps[way])

    def local_rows(q, n):
        return pl.ds(2 * column(q), 2) if n == 0 else pl.ds(group // 2 + column(q), 1)

    def full_local(way, n):
        return same(20 + 2 * way + n, all_local.at[:, local_rows(x, n)], steps[way], 0)

    def half_local(way, n):
        source = (x + 4 - steps[way]) % 4
        return same(
            24 + 2 * way + n, all_local.at[way, local_rows(source, n)], steps[way], 0
        )

    give_leaf = hand(2, leaf_map, all_leaf.at[x, :, y])
    give_a = [
        hand(3 + n, maps.at[:, rows_of], all_local.at[:, local_rows(x, n)])
        for n, rows_of in enumerate((pl.ds(0, 2), pl.ds(2, 1)))
    ]
    top_rows = pl.ds(group - 4, 3)
    give_b = hand(5, maps.at[0, pl.ds(3, 3)], out_local.at[top_rows])
    give_upper = [
        hand(6 + u, upper_maps.at[u], out_upper.at[0, u]) for u in range(UPL)
    ]
    give_top = hand(6 + UPL, top_ref, out_top)
    gifts = [give_b] + give_upper + [give_top]
    low_rows = pl.ds(0, group - 4)

    def leaf_columns(n):
        q = (x + n) % 4
        at = pl.ds(4 * column(q), 4)
        return (
            pltpu.make_async_copy(all_leaf.at[q, 0], out_leaf.at[at], out_sem.at[n]),
            hand(7 + UPL + n, all_leaf.at[q, 1], out_leaf.at[at]),
        )

    def low_levels():
        return (
            pltpu.make_async_copy(
                all_local.at[0], out_local.at[low_rows], out_sem.at[4]
            ),
            hand(11 + UPL, all_local.at[1], out_local.at[low_rows]),
        )

    def peer(r, k):
        pos = w % 4 if r == 0 else quarter
        other = flip(pos, k) if k < 3 else 3 - pos
        cluster = 4 * quarter + other if r == 0 else 4 * other + w % 4
        return pos, on_vec(vec_of(cluster))

    def round_copy(r, k):
        pos, target = peer(r, k)
        return remote(
            quad.at[r, pos],
            quad.at[r, pos],
            ex_send.at[3 * r + k - 1],
            ex_recv.at[3 * r + k - 1],
            target,
        )

    def upper_copy(u):
        branch = (d // (1 << u)) % 2
        return remote(
            joined.at[u - 1, branch],
            joined.at[u - 1, branch],
            ex_send.at[5 + u],
            ex_recv.at[5 + u],
            on_leaf(flip(d, 1 << u)),
        )

    def node(scattered, z, zt):
        size = zt.shape[0]
        z_parts, zt_parts = split(z), split(zt)
        mean_sq = jnp.sum(z * z) / (size * total) + EPSILON
        gram = split(mm3(zt_parts, z_parts))
        interp = mm3(scattered, gram) / (total * mean_sq)
        return interp, mean_sq, zt_parts

    def up_of(interp, mean_sq, zt_parts):
        return mm3(split(interp), zt_parts) * lax.rsqrt(mean_sq)

    def join(left, right):
        zt = jnp.concatenate([left, right], axis=0)
        return jnp.transpose(zt), zt

    def local_weights(g, n):
        return weights[g, n, 0, :, : 2 * rank], weights[g, n, 1, :, : 2 * rank]

    @pl.when(core == 0)
    def _():
        last.start()
        give_leaf.wait_recv()
        for way in range(2):
            full_y(way).start()
        for way in range(2):
            full_x(way, 0).start()
        for came in range(2):
            full_y(came).wait_recv()
            half_y(came).start()
            for way in range(2):
                full_x(way, 1 + came).start()
        for way in range(2):
            full_x(way, 0).wait_recv()
            half_x(way, 0).start()
        for way in range(2):
            half_y(way).wait_recv()
        for way in range(2):
            full_x(way, 3).start()
        for copy in leaf_columns(0):
            copy.start()
        for o in (1, 2):
            for way in range(2):
                full_x(way, o).wait_recv()
                half_x(way, o).start()
        for copy in give_a:
            copy.wait_recv()
        for way in range(2):
            for n in range(2):
                full_local(way, n).start()
        for way in range(2):
            full_x(way, 3).wait_recv()
            half_x(way, 3).start()
        for copy in leaf_columns(1) + leaf_columns(3):
            copy.start()
        for way in range(2):
            for n in range(2):
                full_local(way, n).wait_recv()
                half_local(way, n).start()
        for o in range(4):
            for way in range(2):
                half_x(way, o).wait_recv()
        for copy in leaf_columns(2):
            copy.start()
        for way in range(2):
            for n in range(2):
                half_local(way, n).wait_recv()
        for copy in low_levels():
            copy.start()
        for way in range(2):
            full_y(way).wait_send()
            half_y(way).wait_send()
            for o in range(4):
                full_x(way, o).wait_send()
                half_x(way, o).wait_send()
            for n in range(2):
                full_local(way, n).wait_send()
                half_local(way, n).wait_send()
        for local, across in [leaf_columns(n) for n in range(4)] + [low_levels()]:
            local.wait()
            across.wait_send()
        for copy in gifts:
            copy.wait_recv()
        give_weights.wait_send()
        last.wait_send()

    @pl.when(lead)
    def _():
        z_ref[1, z_rows, :] = sketches[part - 1]
        give_weights.wait_recv()

        @pl.loop(0, part - 1)
        def _(t):
            sketch_copy(t, 1).wait_recv()
            sketch_copy(t, 0).wait_recv()

        last.wait_recv()
        pos = w % 4
        for g in range(2):
            z = z_ref[g]
            made = node((weights[g, 0, 0], weights[g, 0, 1]), z, jnp.transpose(z))
            leaf_map[g] = made[0]
            quad[0, pos, g] = up_of(*made)
        for r in range(2):
            pos = w % 4 if r == 0 else quarter
            branch = pos // 2
            for k in (1, 3, 2):
                round_copy(r, k).start()
            for copy in (give_a if r else [give_leaf]):
                copy.start()
            for which, side in ((0, branch), (1, 1 - branch)):
                for k in ((1,), (2, 3))[which]:
                    round_copy(r, k).wait_recv()
                for g in range(2):
                    z, zt = join(quad[r, 2 * side, g], quad[r, 2 * side + 1, g])
                    made = node(local_weights(g, 1 + 3 * r + side), z, zt)
                    maps[g, 3 * r + side] = made[0]
                    twin[r, side, g] = up_of(*made)
            for g in range(2):
                z, zt = join(twin[r, 0, g], twin[r, 1, g])
                made = node(local_weights(g, 3 + 3 * r), z, zt)
                maps[g, 3 * r + 2] = made[0]
                if r == 0:
                    quad[1, quarter, g] = up_of(*made)
                else:
                    twin[2, 0, g] = up_of(*made)
        give_b.start()
        own_b = pltpu.make_async_copy(
            maps.at[1, pl.ds(3, 3)], out_local.at[top_rows], out_sem.at[0]
        )
        own_b.start()
        z, zt = join(twin[2, 0, 0], twin[2, 0, 1])
        own_upper = []
        for u in range(UPL):
            made = node((upper_weights[u, 0], upper_weights[u, 1]), z, zt)
            upper_maps[u] = made[0]
            if u + 1 < UPL:
                joined[u, (d // (2 << u)) % 2] = up_of(*made)
                upper_copy(u + 1).start()
            give_upper[u].start()
            own_upper.append(
                pltpu.make_async_copy(
                    upper_maps.at[u], out_upper.at[0, u], out_sem.at[1 + u]
                )
            )
            own_upper[-1].start()
            if u + 1 < UPL:
                upper_copy(u + 1).wait_recv()
                z, zt = join(joined[u, 0], joined[u, 1])
            else:
                z_top[...] = z
                kept = z_top[pl.ds(pl.multiple_of(v * columns, columns), columns), :]
                top_ref[0] = mm3(split(kept), split(made[0]), NT) * lax.rsqrt(made[1])
        give_top.start()
        own_top = pltpu.make_async_copy(top_ref, out_top, out_sem.at[1 + UPL])
        own_top.start()
        for copy in [own_b, own_top] + own_upper:
            copy.wait()
        for copy in [give_leaf] + give_a + gifts:
            copy.wait_send()
        for r in range(2):
            for k in range(1, 4):
                round_copy(r, k).wait_send()
        for u in range(1, UPL):
            upper_copy(u).wait_send()
        for _, across in [leaf_columns(n) for n in range(4)] + [low_levels()]:
            across.wait_recv()

    @pl.loop(0, part - 1)
    def _(t):
        sketch_copy(t, core).wait_send()

    for copy in pts_copies + pair_copies + direct + passed(0) + passed(1):
        copy.wait_send()


def write_out(a, b, c, e, out_a, out_b, out_c, out_e, buf_a, buf_b, buf_c, buf_e, in_sem, out_sem):
    pieces = []
    for source, buf, target, step in (
        (a, buf_a, out_a, 4),
        (b, buf_b, out_b, 5),
        (c, buf_c, out_c, 1),
        (e, buf_e, out_e, 1),
    ):
        for start in range(0, source.shape[0], step):
            at = pl.ds(start, step)
            n = len(pieces)
            pieces.append(
                (
                    pltpu.make_async_copy(source.at[at], buf.at[at], in_sem.at[n]),
                    pltpu.make_async_copy(buf.at[at], target.at[at], out_sem.at[n]),
                )
            )
    for arrive, _ in pieces:
        arrive.start()
    for arrive, leave in pieces:
        arrive.wait()
        leave.start()
    for _, leave in pieces:
        leave.wait()


def on_device(
    leaf_n,
    vec_n,
    axes,
    points,
    probe_vectors,
    neighbours,
    leaf_pivots,
    leaf_inverse,
    local_pivots,
    local_inverse,
    upper_pivots,
    upper_inverse,
):
    group, columns, size = probe_vectors.shape
    rank = leaf_pivots.shape[1]
    slots = neighbours.shape[1]
    total = columns * vec_n
    part = group // 2
    pivot_rows = max(p.shape[0] for p in (leaf_pivots, local_pivots, upper_pivots))
    anywhere = pl.BlockSpec(memory_space=pl.ANY)
    hbm = pl.BlockSpec(memory_space=pltpu.HBM)
    dma = pltpu.SemaphoreType.DMA
    shapes = (
        jax.ShapeDtypeStruct((group, rank, size), F32),
        jax.ShapeDtypeStruct((group - 1, rank, 2 * rank), F32),
        jax.ShapeDtypeStruct((1, UPL, rank, 2 * rank), F32),
        jax.ShapeDtypeStruct((1, columns, rank), F32),
    )
    made = pl.pallas_call(
        functools.partial(body, leaf_n, vec_n, axes),
        out_shape=shapes,
        in_specs=[hbm] * 9,
        out_specs=[anywhere] * 4,
        scratch_shapes=[
            pltpu.SMEM((group, slots), jnp.int32),
            pltpu.VMEM((3, -(-pivot_rows // 8) * 8, rank), jnp.int32),
            pltpu.VMEM((3, 3, group, size), BF16),
            pltpu.VMEM((3 * group, 2 * columns, size), BF16),
            pltpu.VMEM((group, 16, size), BF16),
            pltpu.VMEM((3 * group, size, 16), BF16),
            pltpu.VMEM((part, slots * size, size), BF16),
            pltpu.VMEM((2 * columns, slots * size), BF16),
            pltpu.VMEM((7 + UPL, rank, rank), F32),
            pltpu.VMEM((2, 7, 2, rank, size), BF16),
            pltpu.VMEM((UPL, 2, rank, 2 * rank), BF16),
            pltpu.VMEM((part, 2 * columns, size), F32),
            pltpu.VMEM((2, total, size), F32),
            pltpu.VMEM((2, 4, 2, rank, total), F32),
            pltpu.VMEM((3, 2, 2, rank, total), F32),
            pltpu.VMEM((UPL - 1, 2, rank, total), F32),
            pltpu.VMEM((total, 2 * rank), F32),
            pltpu.VMEM((2, rank, size), F32),
            pltpu.VMEM((4, 2, 4, rank, size), F32),
            pltpu.VMEM((2, group - 4, rank, 2 * rank), F32),
            pltpu.VMEM((2, 6, rank, 2 * rank), F32),
            pltpu.VMEM((UPL, rank, 2 * rank), F32),
            pltpu.VMEM((1, columns, rank), F32),
            dma((7 + UPL,)),
            dma((3,)),
            dma((3,)),
            dma((10,)),
            dma((10,)),
            dma((part,)),
            dma((2, part)),
            dma((6 + UPL,)),
            dma((6 + UPL,)),
            dma((12 + UPL,)),
            dma((12 + UPL,)),
            dma((28,)),
            dma((28,)),
            dma((5 + UPL,)),
        ],
        compiler_params=pltpu.CompilerParams(
            collective_id=0, has_side_effects=True, vmem_limit_bytes=60 * 2**20
        ),
    )(
        jnp.transpose(points, (1, 0, 2)),
        probe_vectors,
        neighbours,
        leaf_pivots,
        leaf_inverse,
        local_pivots,
        local_inverse,
        upper_pivots,
        upper_inverse,
    )
    leaf_map, local_map, upper_map, top = pl.pallas_call(
        write_out,
        out_shape=shapes,
        in_specs=[anywhere] * 4,
        out_specs=[hbm] * 4,
        scratch_shapes=[pltpu.VMEM(p.shape, p.dtype) for p in shapes] + [dma((9,))] * 2,
        compiler_params=pltpu.CompilerParams(vmem_limit_bytes=60 * 2**20),
    )(*made)
    return (
        jnp.swapaxes(leaf_map, 1, 2),
        jnp.swapaxes(local_map, 1, 2),
        jnp.swapaxes(upper_map, 2, 3),
        top,
    )


def solution(mesh):
    axes = tuple(mesh.axis_names)
    placed = (
        P("leaf", None, None),
        P("leaf", "vec", None),
        P("leaf", None),
        P("leaf", None),
        P("leaf", None, None),
        P("leaf", None),
        P("leaf", None, None),
        P(),
        P(),
    )
    return jax.shard_map(
        functools.partial(on_device, mesh.shape["leaf"], mesh.shape["vec"], axes),
        mesh=mesh,
        in_specs=placed,
        out_specs=(
            P("leaf", None, None),
            P("leaf", None, None),
            P("leaf", None, None, None),
            P("leaf", "vec", None),
        ),
        check_vma=False,
    )
```

```python
import functools

import jax
import jax.numpy as jnp
from jax import lax
from jax.experimental import pallas as pl
from jax.experimental.pallas import tpu as pltpu
from jax.sharding import PartitionSpec as P

UPL = 3
SOFTEN = 0.0009
EPSILON = 1e-06
F32 = jnp.float32
BF16 = jnp.bfloat16
NN = (((1,), (0,)), ((), ()))
NT = (((1,), (1,)), ((), ()))


def mm(a, b, dims=NN):
    return lax.dot_general(a, b, dims, preferred_element_type=F32)


def split(a):
    high = a.astype(BF16)
    return high, (a - high.astype(F32)).astype(BF16)


def mm3(a, b, dims=NN):
    return mm(a[0], b[0], dims) + (mm(a[0], b[1], dims) + mm(a[1], b[0], dims))


def feature_rows(xyz, weight):
    norm = SOFTEN / 2 + xyz[0] * xyz[0] + xyz[1] * xyz[1] + xyz[2] * xyz[2]
    high = norm.astype(BF16).astype(F32)
    rest = norm - high
    middle = rest.astype(BF16).astype(F32)
    low = (rest - middle).astype(BF16).astype(F32)
    return [part * weight for part in (high, middle, low)]


def body(
    leaf_n,
    vec_n,
    axes,
    pts,
    probe,
    nbr_in,
    leaf_piv,
    leaf_inv,
    local_piv,
    local_inv,
    upper_piv,
    upper_inv,
    out_leaf,
    out_local,
    out_upper,
    out_top,
    nbr,
    piv,
    ext_pts,
    ext_probe,
    near,
    far,
    tiles,
    vectors,
    inv,
    weights,
    upper_weights,
    sketches,
    z_ref,
    quad,
    twin,
    joined,
    z_top,
    leaf_map,
    all_leaf,
    all_local,
    maps,
    upper_maps,
    top_ref,
    inv_sem,
    piv_sem,
    own_sem,
    side_send,
    side_recv,
    sk_send,
    sk_recv,
    ex_send,
    ex_recv,
    mate_send,
    mate_recv,
    map_send,
    map_recv,
    out_sem,
):
    leaf_axis, vec_axis = axes
    d = lax.axis_index(leaf_axis)
    v = lax.axis_index(vec_axis)
    group, columns, points = probe.shape
    rank = inv.shape[1]
    total = columns * vec_n
    wide = 2 * columns
    slots = nbr.shape[1]
    part = group // 2

    x, y = v % 4, v // 4
    pair, side_row = x // 2, x % 2
    half = ((x + 1) // 2) % 2
    w = part * half + 4 * pair + y
    own = w % part
    core = d % 2
    lead = core == 1

    def vec_of(cluster):
        high, low = cluster // part, (cluster // 4) % 2
        return 4 * (cluster % 4) + 2 * low + (high + low) % 2

    def on_vec(u):
        return {leaf_axis: d, vec_axis: u}

    def on_leaf(g):
        return {leaf_axis: g, vec_axis: v}

    def remote(src, dst, send, recv, target):
        return pltpu.make_async_remote_copy(
            src_ref=src,
            dst_ref=dst,
            send_sem=send,
            recv_sem=recv,
            device_id=target,
            device_id_type=pl.DeviceIdType.MESH,
        )

    def flip(index, stride):
        return index + stride * (1 - 2 * ((index // stride) % 2))

    before = (d + leaf_n - 1) % leaf_n
    after = (d + 1) % leaf_n
    mate = flip(d, 1)
    lead_row = d - core + 1

    barrier = pltpu.get_barrier_semaphore()
    targets = []
    for t in range(1, 4):
        row = 4 * ((y + t) % 4)
        targets += [on_vec(u) for u in (4 * y + (x + t) % 4, row + x, row + 3 - x)]
    targets += [on_leaf(g) for g in (before, after, flip(d, 2), flip(d, 4))]
    targets += [
        {leaf_axis: mate, vec_axis: vec_of(half * part + (own + t) % part)}
        for t in range(1, part)
    ]
    for target in targets:
        pl.semaphore_signal(
            barrier, inc=1, device_id=target, device_id_type=pl.DeviceIdType.MESH
        )

    mine = [
        pltpu.make_async_copy(pts, ext_pts.at[1], own_sem.at[0]),
        pltpu.make_async_copy(nbr_in, nbr, own_sem.at[1]),
        pltpu.make_async_copy(
            probe,
            ext_probe.at[
                pl.ds(group, group),
                pl.ds(pl.multiple_of(columns * side_row, columns), columns),
            ],
            own_sem.at[2],
        ),
    ]
    quarter = w // 4
    rows = [(0, leaf_inv, w)]
    rows += [(1, local_inv, 2 * quarter + n) for n in range(2)]
    rows += [(1, local_inv, group // 2 + quarter)]
    rows += [(1, local_inv, group - 4 + n) for n in range(3)]
    local_nodes = len(rows)
    offset = 0
    for u in range(1, UPL + 1):
        rows.append((2, upper_inv, offset + d // (1 << u)))
        offset += leaf_n >> u
    inv_copies = [
        pltpu.make_async_copy(source.at[row], inv.at[n], inv_sem.at[n])
        for n, (_, source, row) in enumerate(rows)
    ]
    piv_copies = [
        pltpu.make_async_copy(
            source, piv.at[n, pl.ds(0, source.shape[0])], piv_sem.at[n]
        )
        for n, source in enumerate((leaf_piv, local_piv, upper_piv))
    ]
    for copy in mine[:1] + piv_copies + inv_copies + mine[1:]:
        copy.start()

    def features(side):
        xyz = [ext_pts[side, c].astype(F32) for c in range(3)]
        norm = feature_rows(xyz, 4096.0)
        one = jnp.ones((1, points), F32)
        pad = jnp.zeros((7, points), F32)
        for r in range(group):
            at = [q[r : r + 1] for q in xyz]
            nm = [q[r : r + 1] for q in norm]
            if side == 1:
                near[r] = jnp.concatenate(at + nm + [one] * 3 + [pad], axis=0).astype(BF16)
            rows_far = [q * -8192.0 for q in at] + [one] * 3 + nm + [pad]
            far[side * group + r] = jnp.transpose(
                jnp.concatenate(rows_far, axis=0)
            ).astype(BF16)

    mine[0].wait()
    features(1)

    for copy in piv_copies:
        copy.wait()
    for n, (which, _, row) in enumerate(rows):
        inv_copies[n].wait()
        size = points if n == 0 else 2 * rank
        chosen = piv[which, pl.ds(row, 1), :]
        spread = (
            lax.broadcasted_iota(jnp.int32, (size, rank), 0) == chosen
        ).astype(F32).astype(BF16)
        for m, piece in enumerate(split(jnp.transpose(inv[n]))):
            scattered = mm(piece, spread, NT).astype(BF16)
            if n < local_nodes:
                weights[core, n, m, :, :size] = scattered
            else:
                upper_weights[n - local_nodes, m] = scattered
    mine[1].wait()
    mine[2].wait()

    pl.semaphore_wait(barrier, len(targets))

    def strip(place, row, piece=None):
        start, count = place * group, group
        if piece is not None:
            start, count = start + piece * part, part
        return ext_probe.at[
            pl.ds(start, count), pl.ds(pl.multiple_of(columns * row, columns), columns)
        ]

    ways = [(after, 0), (before, 2)]
    pts_copies = [
        remote(pts, ext_pts.at[place], side_send.at[n], side_recv.at[n], on_leaf(target))
        for n, (target, place) in enumerate(ways)
    ]
    pair_copies = [
        remote(
            probe.at[pl.ds(piece * part, part)],
            strip(1, side_row, piece),
            side_send.at[2 + piece],
            side_recv.at[2 + piece],
            on_vec(flip(v, 1)),
        )
        for piece in range(2)
    ]
    direct = [
        remote(
            probe,
            strip(place, side_row),
            side_send.at[4 + n],
            side_recv.at[4 + n],
            on_leaf(target),
        )
        for n, (target, place) in enumerate(ways)
    ]

    def passed(piece):
        return [
            remote(
                strip(1, 1 - side_row, piece),
                strip(place, 1 - side_row, piece),
                side_send.at[6 + 2 * piece + n],
                side_recv.at[6 + 2 * piece + n],
                on_leaf(target),
            )
            for n, (target, place) in enumerate(ways)
        ]

    for copy in pts_copies + pair_copies + direct:
        copy.start()

    def hand(n, src, dst):
        return remote(src, dst, mate_send.at[n], mate_recv.at[n], on_leaf(mate))

    give_weights = hand(0, weights.at[0], weights.at[0])

    @pl.when(core == 0)
    def _():
        give_weights.start()

    pts_copies[0].wait_recv()
    features(0)
    pts_copies[1].wait_recv()
    features(2)

    first = (d - 1) * group

    def place_of(c, k):
        listed = nbr[c, k]
        return jnp.clip(listed - first, 0, 3 * group - 1), listed >= 0

    @pl.loop(0, part)
    def _(c):
        cluster = half * part + c
        near_c = near[cluster]
        for k in range(slots):
            place, _ = place_of(cluster, k)
            tiles[c, k * points : (k + 1) * points, :] = lax.rsqrt(
                mm(far[place], near_c)
            ).astype(BF16)
        for piece in range(2):

            @pl.when(c == 2 * piece)
            def _():
                pair_copies[piece].wait_recv()
                for copy in passed(piece):
                    copy.start()

    for copy in direct + passed(0) + passed(1):
        copy.wait_recv()

    z_rows = pl.ds(pl.multiple_of(wide * (2 * y + pair), wide), wide)

    def sketch_copy(t, origin):
        c = half * part + (own + 1 + t) % part
        return remote(
            sketches.at[t],
            z_ref.at[origin, z_rows],
            sk_send.at[t],
            sk_recv.at[origin, t],
            {leaf_axis: lead_row, vec_axis: vec_of(c)},
        )

    last = hand(1, sketches.at[part - 1], z_ref.at[0, z_rows])

    @pl.loop(0, part)
    def _(t):
        c = (own + 1 + t) % part
        for k in range(slots):
            place, listed = place_of(half * part + c, k)
            block = ext_probe[place]
            vectors[:, k * points : (k + 1) * points] = jnp.where(
                listed, block, jnp.zeros_like(block)
            )
        sketches[t] = mm(vectors[...], tiles[c])

        @pl.when(t < part - 1)
        def _():
            sketch_copy(t, core).start()

    def column(q):
        return 2 * (((q + 1) // 2) % 2) + q // 2

    def along(sem, src, dst, step_x, step_y):
        return remote(
            src,
            dst,
            map_send.at[sem],
            map_recv.at[sem],
            on_vec(4 * ((y + step_y) % 4) + (x + step_x) % 4),
        )

    def same(sem, ref, step_x, step_y):
        return along(sem, ref, ref, step_x, step_y)

    steps = (1, 3)
    order = (0, 3, 1, 2)

    def full_x(way):
        return same(16 + way, all_leaf.at[x, :, y], steps[way], 0)

    def half_x(way):
        source = (x + 4 - steps[way]) % 4
        return same(18 + way, all_leaf.at[source, way, y], steps[way], 0)

    def full_y(way, o):
        return same(
            4 * way + o, all_leaf.at[(x + order[o]) % 4, :, y], 0, steps[way]
        )

    def half_y(way, o):
        source = (y + 4 - steps[way]) % 4
        return same(
            8 + 4 * way + o,
            all_leaf.at[(x + order[o]) % 4, way, source],
            0,
            steps[way],
        )

    def local_rows(q, n):
        return pl.ds(2 * column(q), 2) if n == 0 else pl.ds(group // 2 + column(q), 1)

    def full_local(way, n):
        return same(20 + 2 * way + n, all_local.at[:, local_rows(x, n)], steps[way], 0)

    def half_local(way, n):
        source = (x + 4 - steps[way]) % 4
        return same(
            24 + 2 * way + n, all_local.at[way, local_rows(source, n)], steps[way], 0
        )

    give_leaf = hand(2, leaf_map, all_leaf.at[x, :, y])
    give_a = [
        hand(3 + n, maps.at[:, rows_of], all_local.at[:, local_rows(x, n)])
        for n, rows_of in enumerate((pl.ds(0, 2), pl.ds(2, 1)))
    ]
    top_rows = pl.ds(group - 4, 3)
    give_b = hand(5, maps.at[0, pl.ds(3, 3)], out_local.at[top_rows])
    give_upper = [
        hand(6 + u, upper_maps.at[u], out_upper.at[0, u]) for u in range(UPL)
    ]
    give_top = hand(6 + UPL, top_ref, out_top)
    gifts = [give_b] + give_upper + [give_top]
    low_rows = pl.ds(0, group - 4)

    def leaf_columns(n):
        q = (x + n) % 4
        at = pl.ds(4 * column(q), 4)
        return (
            pltpu.make_async_copy(all_leaf.at[q, 0], out_leaf.at[at], out_sem.at[n]),
            hand(7 + UPL + n, all_leaf.at[q, 1], out_leaf.at[at]),
        )

    def low_levels():
        return (
            pltpu.make_async_copy(
                all_local.at[0], out_local.at[low_rows], out_sem.at[4]
            ),
            hand(11 + UPL, all_local.at[1], out_local.at[low_rows]),
        )

    def peer(r, k):
        pos = w % 4 if r == 0 else quarter
        other = flip(pos, k) if k < 3 else 3 - pos
        cluster = 4 * quarter + other if r == 0 else 4 * other + w % 4
        return pos, on_vec(vec_of(cluster))

    def round_copy(r, k):
        pos, target = peer(r, k)
        return remote(
            quad.at[r, pos],
            quad.at[r, pos],
            ex_send.at[3 * r + k - 1],
            ex_recv.at[3 * r + k - 1],
            target,
        )

    def upper_copy(u):
        branch = (d // (1 << u)) % 2
        return remote(
            joined.at[u - 1, branch],
            joined.at[u - 1, branch],
            ex_send.at[5 + u],
            ex_recv.at[5 + u],
            on_leaf(flip(d, 1 << u)),
        )

    def node(scattered, z, zt):
        size = zt.shape[0]
        z_parts, zt_parts = split(z), split(zt)
        mean_sq = jnp.sum(z * z) / (size * total) + EPSILON
        gram = split(mm3(zt_parts, z_parts))
        interp = mm3(scattered, gram) / (total * mean_sq)
        return interp, mean_sq, zt_parts

    def up_of(interp, mean_sq, zt_parts):
        return mm3(split(interp), zt_parts) * lax.rsqrt(mean_sq)

    def join(left, right):
        zt = jnp.concatenate([left, right], axis=0)
        return jnp.transpose(zt), zt

    def local_weights(g, n):
        return weights[g, n, 0, :, : 2 * rank], weights[g, n, 1, :, : 2 * rank]

    @pl.when(core == 0)
    def _():
        last.start()
        give_leaf.wait_recv()
        for way in range(2):
            full_x(way).start()
        for way in range(2):
            full_y(way, 0).start()
        for came in range(2):
            full_x(came).wait_recv()
            half_x(came).start()
            for way in range(2):
                full_y(way, 1 + came).start()
        for way in range(2):
            half_x(way).wait_recv()
        for way in range(2):
            full_y(way, 3).start()
        for way in range(2):
            full_y(way, 0).wait_recv()
            half_y(way, 0).start()
        for copy in give_a:
            copy.wait_recv()
        for way in range(2):
            for n in range(2):
                full_local(way, n).start()
        for o in range(1, 4):
            for way in range(2):
                full_y(way, o).wait_recv()
                half_y(way, o).start()
        for way in range(2):
            for n in range(2):
                full_local(way, n).wait_recv()
                half_local(way, n).start()
        for o in range(4):
            for way in range(2):
                half_y(way, o).wait_recv()
            for copy in leaf_columns(order[o]):
                copy.start()
        for way in range(2):
            for n in range(2):
                half_local(way, n).wait_recv()
        for copy in low_levels():
            copy.start()
        for way in range(2):
            full_x(way).wait_send()
            half_x(way).wait_send()
            for o in range(4):
                full_y(way, o).wait_send()
                half_y(way, o).wait_send()
            for n in range(2):
                full_local(way, n).wait_send()
                half_local(way, n).wait_send()
        for local, across in [leaf_columns(n) for n in range(4)] + [low_levels()]:
            local.wait()
            across.wait_send()
        for copy in gifts:
            copy.wait_recv()
        give_weights.wait_send()
        last.wait_send()

    @pl.when(lead)
    def _():
        z_ref[1, z_rows, :] = sketches[part - 1]
        give_weights.wait_recv()

        @pl.loop(0, part - 1)
        def _(t):
            sketch_copy(t, 1).wait_recv()
            sketch_copy(t, 0).wait_recv()

        last.wait_recv()
        pos = w % 4
        for g in range(2):
            z = z_ref[g]
            made = node((weights[g, 0, 0], weights[g, 0, 1]), z, jnp.transpose(z))
            leaf_map[g] = made[0]
            quad[0, pos, g] = up_of(*made)
        give_leaf.start()
        for r in range(2):
            pos = w % 4 if r == 0 else quarter
            branch = pos // 2
            for k in (1, 3, 2):
                round_copy(r, k).start()
            if r == 1:
                for copy in give_a:
                    copy.start()
            for which, side in ((0, branch), (1, 1 - branch)):
                for k in ((1,), (2, 3))[which]:
                    round_copy(r, k).wait_recv()
                for g in range(2):
                    z, zt = join(quad[r, 2 * side, g], quad[r, 2 * side + 1, g])
                    made = node(local_weights(g, 1 + 3 * r + side), z, zt)
                    maps[g, 3 * r + side] = made[0]
                    twin[r, side, g] = up_of(*made)
            for g in range(2):
                z, zt = join(twin[r, 0, g], twin[r, 1, g])
                made = node(local_weights(g, 3 + 3 * r), z, zt)
                maps[g, 3 * r + 2] = made[0]
                if r == 0:
                    quad[1, quarter, g] = up_of(*made)
                else:
                    twin[2, 0, g] = up_of(*made)
        give_b.start()
        own_b = pltpu.make_async_copy(
            maps.at[1, pl.ds(3, 3)], out_local.at[top_rows], out_sem.at[0]
        )
        own_b.start()
        z, zt = join(twin[2, 0, 0], twin[2, 0, 1])
        own_upper = []
        for u in range(UPL):
            made = node((upper_weights[u, 0], upper_weights[u, 1]), z, zt)
            upper_maps[u] = made[0]
            if u + 1 < UPL:
                joined[u, (d // (2 << u)) % 2] = up_of(*made)
                upper_copy(u + 1).start()
            give_upper[u].start()
            own_upper.append(
                pltpu.make_async_copy(
                    upper_maps.at[u], out_upper.at[0, u], out_sem.at[1 + u]
                )
            )
            own_upper[-1].start()
            if u + 1 < UPL:
                upper_copy(u + 1).wait_recv()
                z, zt = join(joined[u, 0], joined[u, 1])
            else:
                z_top[...] = z
                kept = z_top[pl.ds(pl.multiple_of(v * columns, columns), columns), :]
                top_ref[0] = mm3(split(kept), split(made[0]), NT) * lax.rsqrt(made[1])
        give_top.start()
        own_top = pltpu.make_async_copy(top_ref, out_top, out_sem.at[1 + UPL])
        own_top.start()
        for copy in [own_b, own_top] + own_upper:
            copy.wait()
        for copy in [give_leaf] + give_a + gifts:
            copy.wait_send()
        for r in range(2):
            for k in range(1, 4):
                round_copy(r, k).wait_send()
        for u in range(1, UPL):
            upper_copy(u).wait_send()
        for _, across in [leaf_columns(n) for n in range(4)] + [low_levels()]:
            across.wait_recv()

    @pl.loop(0, part - 1)
    def _(t):
        sketch_copy(t, core).wait_send()

    for copy in pts_copies + pair_copies + direct + passed(0) + passed(1):
        copy.wait_send()


def write_out(a, b, c, e, out_a, out_b, out_c, out_e, buf_a, buf_b, buf_c, buf_e, in_sem, out_sem):
    pieces = []
    for source, buf, target, step in (
        (a, buf_a, out_a, 4),
        (b, buf_b, out_b, 5),
        (c, buf_c, out_c, 1),
        (e, buf_e, out_e, 1),
    ):
        for start in range(0, source.shape[0], step):
            at = pl.ds(start, step)
            n = len(pieces)
            pieces.append(
                (
                    pltpu.make_async_copy(source.at[at], buf.at[at], in_sem.at[n]),
                    pltpu.make_async_copy(buf.at[at], target.at[at], out_sem.at[n]),
                )
            )
    for arrive, _ in pieces:
        arrive.start()
    for arrive, leave in pieces:
        arrive.wait()
        leave.start()
    for _, leave in pieces:
        leave.wait()


def on_device(
    leaf_n,
    vec_n,
    axes,
    points,
    probe_vectors,
    neighbours,
    leaf_pivots,
    leaf_inverse,
    local_pivots,
    local_inverse,
    upper_pivots,
    upper_inverse,
):
    group, columns, size = probe_vectors.shape
    rank = leaf_pivots.shape[1]
    slots = neighbours.shape[1]
    total = columns * vec_n
    part = group // 2
    pivot_rows = max(p.shape[0] for p in (leaf_pivots, local_pivots, upper_pivots))
    anywhere = pl.BlockSpec(memory_space=pl.ANY)
    hbm = pl.BlockSpec(memory_space=pltpu.HBM)
    dma = pltpu.SemaphoreType.DMA
    shapes = (
        jax.ShapeDtypeStruct((group, rank, size), F32),
        jax.ShapeDtypeStruct((group - 1, rank, 2 * rank), F32),
        jax.ShapeDtypeStruct((1, UPL, rank, 2 * rank), F32),
        jax.ShapeDtypeStruct((1, columns, rank), F32),
    )
    made = pl.pallas_call(
        functools.partial(body, leaf_n, vec_n, axes),
        out_shape=shapes,
        in_specs=[hbm] * 9,
        out_specs=[anywhere] * 4,
        scratch_shapes=[
            pltpu.SMEM((group, slots), jnp.int32),
            pltpu.VMEM((3, -(-pivot_rows // 8) * 8, rank), jnp.int32),
            pltpu.VMEM((3, 3, group, size), BF16),
            pltpu.VMEM((3 * group, 2 * columns, size), BF16),
            pltpu.VMEM((group, 16, size), BF16),
            pltpu.VMEM((3 * group, size, 16), BF16),
            pltpu.VMEM((part, slots * size, size), BF16),
            pltpu.VMEM((2 * columns, slots * size), BF16),
            pltpu.VMEM((7 + UPL, rank, rank), F32),
            pltpu.VMEM((2, 7, 2, rank, size), BF16),
            pltpu.VMEM((UPL, 2, rank, 2 * rank), BF16),
            pltpu.VMEM((part, 2 * columns, size), F32),
            pltpu.VMEM((2, total, size), F32),
            pltpu.VMEM((2, 4, 2, rank, total), F32),
            pltpu.VMEM((3, 2, 2, rank, total), F32),
            pltpu.VMEM((UPL - 1, 2, rank, total), F32),
            pltpu.VMEM((total, 2 * rank), F32),
            pltpu.VMEM((2, rank, size), F32),
            pltpu.VMEM((4, 2, 4, rank, size), F32),
            pltpu.VMEM((2, group - 4, rank, 2 * rank), F32),
            pltpu.VMEM((2, 6, rank, 2 * rank), F32),
            pltpu.VMEM((UPL, rank, 2 * rank), F32),
            pltpu.VMEM((1, columns, rank), F32),
            dma((7 + UPL,)),
            dma((3,)),
            dma((3,)),
            dma((10,)),
            dma((10,)),
            dma((part,)),
            dma((2, part)),
            dma((6 + UPL,)),
            dma((6 + UPL,)),
            dma((12 + UPL,)),
            dma((12 + UPL,)),
            dma((28,)),
            dma((28,)),
            dma((5 + UPL,)),
        ],
        compiler_params=pltpu.CompilerParams(
            collective_id=0, has_side_effects=True, vmem_limit_bytes=60 * 2**20
        ),
    )(
        jnp.transpose(points, (1, 0, 2)),
        probe_vectors,
        neighbours,
        leaf_pivots,
        leaf_inverse,
        local_pivots,
        local_inverse,
        upper_pivots,
        upper_inverse,
    )
    leaf_map, local_map, upper_map, top = pl.pallas_call(
        write_out,
        out_shape=shapes,
        in_specs=[anywhere] * 4,
        out_specs=[hbm] * 4,
        scratch_shapes=[pltpu.VMEM(p.shape, p.dtype) for p in shapes] + [dma((9,))] * 2,
        compiler_params=pltpu.CompilerParams(vmem_limit_bytes=60 * 2**20),
    )(*made)
    return (
        jnp.swapaxes(leaf_map, 1, 2),
        jnp.swapaxes(local_map, 1, 2),
        jnp.swapaxes(upper_map, 2, 3),
        top,
    )


def solution(mesh):
    axes = tuple(mesh.axis_names)
    placed = (
        P("leaf", None, None),
        P("leaf", "vec", None),
        P("leaf", None),
        P("leaf", None),
        P("leaf", None, None),
        P("leaf", None),
        P("leaf", None, None),
        P(),
        P(),
    )
    return jax.shard_map(
        functools.partial(on_device, mesh.shape["leaf"], mesh.shape["vec"], axes),
        mesh=mesh,
        in_specs=placed,
        out_specs=(
            P("leaf", None, None),
            P("leaf", None, None),
            P("leaf", None, None, None),
            P("leaf", "vec", None),
        ),
        check_vma=False,
    )
```

```python
import functools

import jax
import jax.numpy as jnp
from jax import lax
from jax.experimental import pallas as pl
from jax.experimental.pallas import tpu as pltpu
from jax.sharding import PartitionSpec as P

UPL = 3
SOFTEN = 0.0009
EPSILON = 1e-06
F32 = jnp.float32
BF16 = jnp.bfloat16
NN = (((1,), (0,)), ((), ()))
NT = (((1,), (1,)), ((), ()))


def mm(a, b, dims=NN):
    return lax.dot_general(a, b, dims, preferred_element_type=F32)


def split(a):
    high = a.astype(BF16)
    return high, (a - high.astype(F32)).astype(BF16)


def mm3(a, b, dims=NN):
    return mm(a[0], b[0], dims) + (mm(a[0], b[1], dims) + mm(a[1], b[0], dims))


def feature_rows(xyz, weight):
    norm = SOFTEN / 2 + xyz[0] * xyz[0] + xyz[1] * xyz[1] + xyz[2] * xyz[2]
    high = norm.astype(BF16).astype(F32)
    rest = norm - high
    middle = rest.astype(BF16).astype(F32)
    low = (rest - middle).astype(BF16).astype(F32)
    return [part * weight for part in (high, middle, low)]


def body(
    leaf_n,
    vec_n,
    axes,
    pts,
    probe,
    nbr_in,
    leaf_piv,
    leaf_inv,
    local_piv,
    local_inv,
    upper_piv,
    upper_inv,
    out_leaf,
    out_local,
    out_upper,
    out_top,
    nbr,
    piv,
    ext_pts,
    ext_probe,
    near,
    far,
    tiles,
    vectors,
    inv,
    weights,
    upper_weights,
    sketches,
    z_ref,
    quad,
    twin,
    joined,
    z_top,
    leaf_map,
    all_leaf,
    all_local,
    maps,
    upper_maps,
    top_ref,
    inv_sem,
    piv_sem,
    own_sem,
    side_send,
    side_recv,
    sk_send,
    sk_recv,
    ex_send,
    ex_recv,
    mate_send,
    mate_recv,
    map_send,
    map_recv,
    out_sem,
):
    leaf_axis, vec_axis = axes
    d = lax.axis_index(leaf_axis)
    v = lax.axis_index(vec_axis)
    group, columns, points = probe.shape
    rank = inv.shape[1]
    total = columns * vec_n
    wide = 2 * columns
    slots = nbr.shape[1]
    part = group // 2

    x, y = v % 4, v // 4
    pair, side_row = x // 2, x % 2
    half = ((x + 1) // 2) % 2
    w = part * half + 4 * pair + y
    own = w % part
    core = d % 2
    lead = core == 1

    def vec_of(cluster):
        high, low = cluster // part, (cluster // 4) % 2
        return 4 * (cluster % 4) + 2 * low + (high + low) % 2

    def on_vec(u):
        return {leaf_axis: d, vec_axis: u}

    def on_leaf(g):
        return {leaf_axis: g, vec_axis: v}

    def remote(src, dst, send, recv, target):
        return pltpu.make_async_remote_copy(
            src_ref=src,
            dst_ref=dst,
            send_sem=send,
            recv_sem=recv,
            device_id=target,
            device_id_type=pl.DeviceIdType.MESH,
        )

    def flip(index, stride):
        return index + stride * (1 - 2 * ((index // stride) % 2))

    before = (d + leaf_n - 1) % leaf_n
    after = (d + 1) % leaf_n
    mate = flip(d, 1)
    lead_row = d - core + 1

    barrier = pltpu.get_barrier_semaphore()
    targets = []
    for t in range(1, 4):
        row = 4 * ((y + t) % 4)
        targets += [on_vec(u) for u in (4 * y + (x + t) % 4, row + x, row + 3 - x)]
    targets += [on_leaf(g) for g in (before, after, flip(d, 2), flip(d, 4))]
    targets += [
        {leaf_axis: mate, vec_axis: vec_of(half * part + (own + t) % part)}
        for t in range(1, part)
    ]
    for target in targets:
        pl.semaphore_signal(
            barrier, inc=1, device_id=target, device_id_type=pl.DeviceIdType.MESH
        )

    mine = [
        pltpu.make_async_copy(pts, ext_pts.at[1], own_sem.at[0]),
        pltpu.make_async_copy(nbr_in, nbr, own_sem.at[1]),
        pltpu.make_async_copy(
            probe,
            ext_probe.at[
                pl.ds(group, group),
                pl.ds(pl.multiple_of(columns * side_row, columns), columns),
            ],
            own_sem.at[2],
        ),
    ]
    quarter = w // 4
    rows = [(0, leaf_inv, w)]
    rows += [(1, local_inv, 2 * quarter + n) for n in range(2)]
    rows += [(1, local_inv, group // 2 + quarter)]
    rows += [(1, local_inv, group - 4 + n) for n in range(3)]
    local_nodes = len(rows)
    offset = 0
    for u in range(1, UPL + 1):
        rows.append((2, upper_inv, offset + d // (1 << u)))
        offset += leaf_n >> u
    inv_copies = [
        pltpu.make_async_copy(source.at[row], inv.at[n], inv_sem.at[n])
        for n, (_, source, row) in enumerate(rows)
    ]
    piv_copies = [
        pltpu.make_async_copy(
            source, piv.at[n, pl.ds(0, source.shape[0])], piv_sem.at[n]
        )
        for n, source in enumerate((leaf_piv, local_piv, upper_piv))
    ]
    for copy in mine[:1] + piv_copies + inv_copies + mine[1:]:
        copy.start()

    def features(side):
        xyz = [ext_pts[side, c].astype(F32) for c in range(3)]
        norm = feature_rows(xyz, 4096.0)
        one = jnp.ones((1, points), F32)
        pad = jnp.zeros((7, points), F32)
        for r in range(group):
            at = [q[r : r + 1] for q in xyz]
            nm = [q[r : r + 1] for q in norm]
            if side == 1:
                near[r] = jnp.concatenate(at + nm + [one] * 3 + [pad], axis=0).astype(BF16)
            rows_far = [q * -8192.0 for q in at] + [one] * 3 + nm + [pad]
            far[side * group + r] = jnp.transpose(
                jnp.concatenate(rows_far, axis=0)
            ).astype(BF16)

    mine[0].wait()
    features(1)

    for copy in piv_copies:
        copy.wait()
    for n, (which, _, row) in enumerate(rows):
        inv_copies[n].wait()
        size = points if n == 0 else 2 * rank
        chosen = piv[which, pl.ds(row, 1), :]
        spread = (
            lax.broadcasted_iota(jnp.int32, (size, rank), 0) == chosen
        ).astype(F32).astype(BF16)
        for m, piece in enumerate(split(jnp.transpose(inv[n]))):
            scattered = mm(piece, spread, NT).astype(BF16)
            if n < local_nodes:
                weights[core, n, m, :, :size] = scattered
            else:
                upper_weights[n - local_nodes, m] = scattered
    mine[1].wait()
    mine[2].wait()

    pl.semaphore_wait(barrier, len(targets))

    def strip(place, row, piece=None):
        start, count = place * group, group
        if piece is not None:
            start, count = start + piece * part, part
        return ext_probe.at[
            pl.ds(start, count), pl.ds(pl.multiple_of(columns * row, columns), columns)
        ]

    ways = [(after, 0), (before, 2)]
    pts_copies = [
        remote(pts, ext_pts.at[place], side_send.at[n], side_recv.at[n], on_leaf(target))
        for n, (target, place) in enumerate(ways)
    ]
    pair_copies = [
        remote(
            probe.at[pl.ds(piece * part, part)],
            strip(1, side_row, piece),
            side_send.at[2 + piece],
            side_recv.at[2 + piece],
            on_vec(flip(v, 1)),
        )
        for piece in range(2)
    ]
    direct = [
        remote(
            probe,
            strip(place, side_row),
            side_send.at[4 + n],
            side_recv.at[4 + n],
            on_leaf(target),
        )
        for n, (target, place) in enumerate(ways)
    ]

    def passed(piece):
        return [
            remote(
                strip(1, 1 - side_row, piece),
                strip(place, 1 - side_row, piece),
                side_send.at[6 + 2 * piece + n],
                side_recv.at[6 + 2 * piece + n],
                on_leaf(target),
            )
            for n, (target, place) in enumerate(ways)
        ]

    for copy in pts_copies + pair_copies + direct:
        copy.start()

    def hand(n, src, dst):
        return remote(src, dst, mate_send.at[n], mate_recv.at[n], on_leaf(mate))

    give_weights = hand(0, weights.at[0], weights.at[0])

    @pl.when(core == 0)
    def _():
        give_weights.start()

    def tile(place, cluster):
        return lax.rsqrt(mm(far[place], near[cluster])).astype(BF16)

    for c in range(part):
        cluster = half * part + c
        tiles[c, :points, :] = tile(group + cluster, cluster)

    pts_copies[0].wait_recv()
    features(0)
    pts_copies[1].wait_recv()
    features(2)

    first = (d - 1) * group

    def place_of(c, k):
        listed = nbr[c, k]
        return jnp.clip(listed - first, 0, 3 * group - 1), listed >= 0

    @pl.loop(0, part)
    def _(c):
        cluster = half * part + c
        for k in range(1, slots):
            place, _ = place_of(cluster, k)
            tiles[c, k * points : (k + 1) * points, :] = tile(place, cluster)
        for piece in range(2):

            @pl.when(c == 2 * piece)
            def _():
                pair_copies[piece].wait_recv()
                for copy in passed(piece):
                    copy.start()

    for copy in direct + passed(0) + passed(1):
        copy.wait_recv()

    z_rows = pl.ds(pl.multiple_of(wide * (2 * y + pair), wide), wide)

    def sketch_copy(t, origin):
        c = half * part + (own + 1 + t) % part
        return remote(
            sketches.at[t],
            z_ref.at[origin, z_rows],
            sk_send.at[t],
            sk_recv.at[origin, t],
            {leaf_axis: lead_row, vec_axis: vec_of(c)},
        )

    last = hand(1, sketches.at[part - 1], z_ref.at[0, z_rows])

    @pl.loop(0, part)
    def _(t):
        c = (own + 1 + t) % part
        for k in range(slots):
            place, listed = place_of(half * part + c, k)
            block = ext_probe[place]
            vectors[:, k * points : (k + 1) * points] = jnp.where(
                listed, block, jnp.zeros_like(block)
            )
        sketches[t] = mm(vectors[...], tiles[c])

        @pl.when(t < part - 1)
        def _():
            sketch_copy(t, core).start()

    def column(q):
        return 2 * (((q + 1) // 2) % 2) + q // 2

    def along(sem, src, dst, step_x, step_y):
        return remote(
            src,
            dst,
            map_send.at[sem],
            map_recv.at[sem],
            on_vec(4 * ((y + step_y) % 4) + (x + step_x) % 4),
        )

    def same(sem, ref, step_x, step_y):
        return along(sem, ref, ref, step_x, step_y)

    steps = (1, 3)
    order = (0, 3, 1, 2)

    def full_x(way):
        return same(16 + way, all_leaf.at[x, :, y], steps[way], 0)

    def half_x(way):
        source = (x + 4 - steps[way]) % 4
        return same(18 + way, all_leaf.at[source, way, y], steps[way], 0)

    def full_y(way, o):
        return same(
            4 * way + o, all_leaf.at[(x + order[o]) % 4, :, y], 0, steps[way]
        )

    def half_y(way, o):
        source = (y + 4 - steps[way]) % 4
        return same(
            8 + 4 * way + o,
            all_leaf.at[(x + order[o]) % 4, way, source],
            0,
            steps[way],
        )

    def local_rows(q, n):
        return pl.ds(2 * column(q), 2) if n == 0 else pl.ds(group // 2 + column(q), 1)

    def full_local(way, n):
        return same(20 + 2 * way + n, all_local.at[:, local_rows(x, n)], steps[way], 0)

    def half_local(way, n):
        source = (x + 4 - steps[way]) % 4
        return same(
            24 + 2 * way + n, all_local.at[way, local_rows(source, n)], steps[way], 0
        )

    give_leaf = hand(2, leaf_map, all_leaf.at[x, :, y])
    give_a = [
        hand(3 + n, maps.at[:, rows_of], all_local.at[:, local_rows(x, n)])
        for n, rows_of in enumerate((pl.ds(0, 2), pl.ds(2, 1)))
    ]
    top_rows = pl.ds(group - 4, 3)
    give_b = hand(5, maps.at[0, pl.ds(3, 3)], out_local.at[top_rows])
    give_upper = [
        hand(6 + u, upper_maps.at[u], out_upper.at[0, u]) for u in range(UPL)
    ]
    give_top = hand(6 + UPL, top_ref, out_top)
    gifts = [give_b] + give_upper + [give_top]
    low_rows = pl.ds(0, group - 4)

    def leaf_columns(n):
        q = (x + n) % 4
        at = pl.ds(4 * column(q), 4)
        return (
            pltpu.make_async_copy(all_leaf.at[q, 0], out_leaf.at[at], out_sem.at[n]),
            hand(7 + UPL + n, all_leaf.at[q, 1], out_leaf.at[at]),
        )

    def low_levels():
        return (
            pltpu.make_async_copy(
                all_local.at[0], out_local.at[low_rows], out_sem.at[4]
            ),
            hand(11 + UPL, all_local.at[1], out_local.at[low_rows]),
        )

    def peer(r, k):
        pos = w % 4 if r == 0 else quarter
        other = flip(pos, k) if k < 3 else 3 - pos
        cluster = 4 * quarter + other if r == 0 else 4 * other + w % 4
        return pos, on_vec(vec_of(cluster))

    def round_copy(r, k):
        pos, target = peer(r, k)
        return remote(
            quad.at[r, pos],
            quad.at[r, pos],
            ex_send.at[3 * r + k - 1],
            ex_recv.at[3 * r + k - 1],
            target,
        )

    def upper_copy(u):
        branch = (d // (1 << u)) % 2
        return remote(
            joined.at[u - 1, branch],
            joined.at[u - 1, branch],
            ex_send.at[5 + u],
            ex_recv.at[5 + u],
            on_leaf(flip(d, 1 << u)),
        )

    def nodes(items):
        parts = [split(zt) for _, zt in items]
        mean_sq = [
            jnp.sum(zt * zt) / (zt.shape[0] * total) + EPSILON for _, zt in items
        ]
        grams = [split(mm3(p, p, NT)) for p in parts]
        return [
            (mm3(scattered, gram) / (total * m), m, p)
            for (scattered, _), gram, m, p in zip(items, grams, mean_sq, parts)
        ]

    def ups(made):
        interps = [split(interp) for interp, _, _ in made]
        return [
            mm3(interp, p) * lax.rsqrt(m) for interp, (_, m, p) in zip(interps, made)
        ]

    def join(left, right):
        return jnp.concatenate([left, right], axis=0)

    def local_weights(g, n):
        return weights[g, n, 0, :, : 2 * rank], weights[g, n, 1, :, : 2 * rank]

    @pl.when(core == 0)
    def _():
        last.start()
        give_leaf.wait_recv()
        for way in range(2):
            full_x(way).start()
        for way in range(2):
            full_y(way, 0).start()
        for came in range(2):
            full_x(came).wait_recv()
            half_x(came).start()
            for way in range(2):
                full_y(way, 1 + came).start()
        for way in range(2):
            half_x(way).wait_recv()
        for way in range(2):
            full_y(way, 3).start()
        for way in range(2):
            full_y(way, 0).wait_recv()
            half_y(way, 0).start()
        for copy in give_a:
            copy.wait_recv()
        for way in range(2):
            for n in range(2):
                full_local(way, n).start()
        for o in range(1, 4):
            for way in range(2):
                full_y(way, o).wait_recv()
                half_y(way, o).start()
        for way in range(2):
            for n in range(2):
                full_local(way, n).wait_recv()
                half_local(way, n).start()
        for o in range(4):
            for way in range(2):
                half_y(way, o).wait_recv()
            for copy in leaf_columns(order[o]):
                copy.start()
        for way in range(2):
            for n in range(2):
                half_local(way, n).wait_recv()
        for copy in low_levels():
            copy.start()
        for way in range(2):
            full_x(way).wait_send()
            half_x(way).wait_send()
            for o in range(4):
                full_y(way, o).wait_send()
                half_y(way, o).wait_send()
            for n in range(2):
                full_local(way, n).wait_send()
                half_local(way, n).wait_send()
        for local, across in [leaf_columns(n) for n in range(4)] + [low_levels()]:
            local.wait()
            across.wait_send()
        for copy in gifts:
            copy.wait_recv()
        give_weights.wait_send()
        last.wait_send()

    @pl.when(lead)
    def _():
        z_ref[1, z_rows, :] = sketches[part - 1]
        give_weights.wait_recv()

        @pl.loop(0, part - 1)
        def _(t):
            sketch_copy(t, 1).wait_recv()
            sketch_copy(t, 0).wait_recv()

        last.wait_recv()
        pos = w % 4
        made = nodes(
            [
                ((weights[g, 0, 0], weights[g, 0, 1]), jnp.transpose(z_ref[g]))
                for g in range(2)
            ]
        )
        raised = ups(made)
        for g in range(2):
            leaf_map[g] = made[g][0]
            quad[0, pos, g] = raised[g]
        give_leaf.start()
        for r in range(2):
            pos = w % 4 if r == 0 else quarter
            branch = pos // 2
            for k in (1, 3, 2):
                round_copy(r, k).start()
            if r == 1:
                for copy in give_a:
                    copy.start()
            for which, side in ((0, branch), (1, 1 - branch)):
                for k in ((1,), (2, 3))[which]:
                    round_copy(r, k).wait_recv()
                made = nodes(
                    [
                        (
                            local_weights(g, 1 + 3 * r + side),
                            join(quad[r, 2 * side, g], quad[r, 2 * side + 1, g]),
                        )
                        for g in range(2)
                    ]
                )
                raised = ups(made)
                for g in range(2):
                    maps[g, 3 * r + side] = made[g][0]
                    twin[r, side, g] = raised[g]
            made = nodes(
                [
                    (local_weights(g, 3 + 3 * r), join(twin[r, 0, g], twin[r, 1, g]))
                    for g in range(2)
                ]
            )
            raised = ups(made)
            for g in range(2):
                maps[g, 3 * r + 2] = made[g][0]
                if r == 0:
                    quad[1, quarter, g] = raised[g]
        give_b.start()
        own_b = pltpu.make_async_copy(
            maps.at[1, pl.ds(3, 3)], out_local.at[top_rows], out_sem.at[0]
        )
        own_b.start()
        zt = join(*raised)
        own_upper = []
        for u in range(UPL):
            made = nodes([((upper_weights[u, 0], upper_weights[u, 1]), zt)])
            interp, mean_sq, _ = made[0]
            upper_maps[u] = interp
            if u + 1 < UPL:
                joined[u, (d // (2 << u)) % 2] = ups(made)[0]
                upper_copy(u + 1).start()
            give_upper[u].start()
            own_upper.append(
                pltpu.make_async_copy(
                    upper_maps.at[u], out_upper.at[0, u], out_sem.at[1 + u]
                )
            )
            own_upper[-1].start()
            if u + 1 < UPL:
                upper_copy(u + 1).wait_recv()
                zt = join(joined[u, 0], joined[u, 1])
            else:
                z_top[...] = jnp.transpose(zt)
                kept = z_top[pl.ds(pl.multiple_of(v * columns, columns), columns), :]
                top_ref[0] = mm3(split(kept), split(interp), NT) * lax.rsqrt(mean_sq)
        give_top.start()
        own_top = pltpu.make_async_copy(top_ref, out_top, out_sem.at[1 + UPL])
        own_top.start()
        for copy in [own_b, own_top] + own_upper:
            copy.wait()
        for copy in [give_leaf] + give_a + gifts:
            copy.wait_send()
        for r in range(2):
            for k in range(1, 4):
                round_copy(r, k).wait_send()
        for u in range(1, UPL):
            upper_copy(u).wait_send()
        for _, across in [leaf_columns(n) for n in range(4)] + [low_levels()]:
            across.wait_recv()

    @pl.loop(0, part - 1)
    def _(t):
        sketch_copy(t, core).wait_send()

    for copy in pts_copies + pair_copies + direct + passed(0) + passed(1):
        copy.wait_send()


def write_out(a, b, c, e, out_a, out_b, out_c, out_e, buf_a, buf_b, buf_c, buf_e, in_sem, out_sem):
    pieces = []
    for source, buf, target, step in (
        (a, buf_a, out_a, 4),
        (b, buf_b, out_b, 5),
        (c, buf_c, out_c, 1),
        (e, buf_e, out_e, 1),
    ):
        for start in range(0, source.shape[0], step):
            at = pl.ds(start, step)
            n = len(pieces)
            pieces.append(
                (
                    pltpu.make_async_copy(source.at[at], buf.at[at], in_sem.at[n]),
                    pltpu.make_async_copy(buf.at[at], target.at[at], out_sem.at[n]),
                )
            )
    for arrive, _ in pieces:
        arrive.start()
    for arrive, leave in pieces:
        arrive.wait()
        leave.start()
    for _, leave in pieces:
        leave.wait()


def on_device(
    leaf_n,
    vec_n,
    axes,
    points,
    probe_vectors,
    neighbours,
    leaf_pivots,
    leaf_inverse,
    local_pivots,
    local_inverse,
    upper_pivots,
    upper_inverse,
):
    group, columns, size = probe_vectors.shape
    rank = leaf_pivots.shape[1]
    slots = neighbours.shape[1]
    total = columns * vec_n
    part = group // 2
    pivot_rows = max(p.shape[0] for p in (leaf_pivots, local_pivots, upper_pivots))
    anywhere = pl.BlockSpec(memory_space=pl.ANY)
    hbm = pl.BlockSpec(memory_space=pltpu.HBM)
    dma = pltpu.SemaphoreType.DMA
    shapes = (
        jax.ShapeDtypeStruct((group, rank, size), F32),
        jax.ShapeDtypeStruct((group - 1, rank, 2 * rank), F32),
        jax.ShapeDtypeStruct((1, UPL, rank, 2 * rank), F32),
        jax.ShapeDtypeStruct((1, columns, rank), F32),
    )
    made = pl.pallas_call(
        functools.partial(body, leaf_n, vec_n, axes),
        out_shape=shapes,
        in_specs=[hbm] * 9,
        out_specs=[anywhere] * 4,
        scratch_shapes=[
            pltpu.SMEM((group, slots), jnp.int32),
            pltpu.VMEM((3, -(-pivot_rows // 8) * 8, rank), jnp.int32),
            pltpu.VMEM((3, 3, group, size), BF16),
            pltpu.VMEM((3 * group, 2 * columns, size), BF16),
            pltpu.VMEM((group, 16, size), BF16),
            pltpu.VMEM((3 * group, size, 16), BF16),
            pltpu.VMEM((part, slots * size, size), BF16),
            pltpu.VMEM((2 * columns, slots * size), BF16),
            pltpu.VMEM((7 + UPL, rank, rank), F32),
            pltpu.VMEM((2, 7, 2, rank, size), BF16),
            pltpu.VMEM((UPL, 2, rank, 2 * rank), BF16),
            pltpu.VMEM((part, 2 * columns, size), F32),
            pltpu.VMEM((2, total, size), F32),
            pltpu.VMEM((2, 4, 2, rank, total), F32),
            pltpu.VMEM((2, 2, 2, rank, total), F32),
            pltpu.VMEM((UPL - 1, 2, rank, total), F32),
            pltpu.VMEM((total, 2 * rank), F32),
            pltpu.VMEM((2, rank, size), F32),
            pltpu.VMEM((4, 2, 4, rank, size), F32),
            pltpu.VMEM((2, group - 4, rank, 2 * rank), F32),
            pltpu.VMEM((2, 6, rank, 2 * rank), F32),
            pltpu.VMEM((UPL, rank, 2 * rank), F32),
            pltpu.VMEM((1, columns, rank), F32),
            dma((7 + UPL,)),
            dma((3,)),
            dma((3,)),
            dma((10,)),
            dma((10,)),
            dma((part,)),
            dma((2, part)),
            dma((6 + UPL,)),
            dma((6 + UPL,)),
            dma((12 + UPL,)),
            dma((12 + UPL,)),
            dma((28,)),
            dma((28,)),
            dma((5 + UPL,)),
        ],
        compiler_params=pltpu.CompilerParams(
            collective_id=0, has_side_effects=True, vmem_limit_bytes=60 * 2**20
        ),
    )(
        jnp.transpose(points, (1, 0, 2)),
        probe_vectors,
        neighbours,
        leaf_pivots,
        leaf_inverse,
        local_pivots,
        local_inverse,
        upper_pivots,
        upper_inverse,
    )
    leaf_map, local_map, upper_map, top = pl.pallas_call(
        write_out,
        out_shape=shapes,
        in_specs=[anywhere] * 4,
        out_specs=[hbm] * 4,
        scratch_shapes=[pltpu.VMEM(p.shape, p.dtype) for p in shapes] + [dma((9,))] * 2,
        compiler_params=pltpu.CompilerParams(vmem_limit_bytes=60 * 2**20),
    )(*made)
    return (
        jnp.swapaxes(leaf_map, 1, 2),
        jnp.swapaxes(local_map, 1, 2),
        jnp.swapaxes(upper_map, 2, 3),
        top,
    )


def solution(mesh):
    axes = tuple(mesh.axis_names)
    placed = (
        P("leaf", None, None),
        P("leaf", "vec", None),
        P("leaf", None),
        P("leaf", None),
        P("leaf", None, None),
        P("leaf", None),
        P("leaf", None, None),
        P(),
        P(),
    )
    return jax.shard_map(
        functools.partial(on_device, mesh.shape["leaf"], mesh.shape["vec"], axes),
        mesh=mesh,
        in_specs=placed,
        out_specs=(
            P("leaf", None, None),
            P("leaf", None, None),
            P("leaf", None, None, None),
            P("leaf", "vec", None),
        ),
        check_vma=False,
    )
```

```python
import functools

import jax
import jax.numpy as jnp
from jax import lax
from jax.experimental import pallas as pl
from jax.experimental.pallas import tpu as pltpu
from jax.sharding import PartitionSpec as P

UPL = 3
SOFTEN = 0.0009
EPSILON = 1e-06
F32 = jnp.float32
BF16 = jnp.bfloat16
NN = (((1,), (0,)), ((), ()))
NT = (((1,), (1,)), ((), ()))


def mm(a, b, dims=NN):
    return lax.dot_general(a, b, dims, preferred_element_type=F32)


def split(a):
    high = a.astype(BF16)
    return high, (a - high.astype(F32)).astype(BF16)


def mm3(a, b, dims=NN):
    return mm(a[0], b[0], dims) + (mm(a[0], b[1], dims) + mm(a[1], b[0], dims))


def feature_rows(xyz, weight):
    norm = SOFTEN / 2 + xyz[0] * xyz[0] + xyz[1] * xyz[1] + xyz[2] * xyz[2]
    high = norm.astype(BF16).astype(F32)
    rest = norm - high
    middle = rest.astype(BF16).astype(F32)
    low = (rest - middle).astype(BF16).astype(F32)
    return [part * weight for part in (high, middle, low)]


def body(
    leaf_n,
    vec_n,
    axes,
    pts,
    probe,
    nbr_in,
    leaf_piv,
    leaf_inv,
    local_piv,
    local_inv,
    upper_piv,
    upper_inv,
    out_leaf,
    out_local,
    out_upper,
    out_top,
    nbr,
    piv,
    ext_pts,
    ext_probe,
    near,
    far,
    tiles,
    vectors,
    inv,
    weights,
    upper_weights,
    sketches,
    z_ref,
    quad,
    twin,
    joined,
    z_top,
    leaf_map,
    all_leaf,
    all_local,
    maps,
    upper_maps,
    top_ref,
    inv_sem,
    piv_sem,
    own_sem,
    side_send,
    side_recv,
    sk_send,
    sk_recv,
    ex_send,
    ex_recv,
    mate_send,
    mate_recv,
    map_send,
    map_recv,
    out_sem,
):
    leaf_axis, vec_axis = axes
    d = lax.axis_index(leaf_axis)
    v = lax.axis_index(vec_axis)
    group, columns, points = probe.shape
    rank = inv.shape[1]
    total = columns * vec_n
    wide = 2 * columns
    slots = nbr.shape[1]
    part = group // 2

    x, y = v % 4, v // 4
    pair, side_row = x // 2, x % 2
    half = ((x + 1) // 2) % 2
    w = part * half + 4 * pair + y
    own = w % part
    core = d % 2
    lead = core == 1

    def vec_of(cluster):
        high, low = cluster // part, (cluster // 4) % 2
        return 4 * (cluster % 4) + 2 * low + (high + low) % 2

    def on_vec(u):
        return {leaf_axis: d, vec_axis: u}

    def on_leaf(g):
        return {leaf_axis: g, vec_axis: v}

    def remote(src, dst, send, recv, target):
        return pltpu.make_async_remote_copy(
            src_ref=src,
            dst_ref=dst,
            send_sem=send,
            recv_sem=recv,
            device_id=target,
            device_id_type=pl.DeviceIdType.MESH,
        )

    def flip(index, stride):
        return index + stride * (1 - 2 * ((index // stride) % 2))

    before = (d + leaf_n - 1) % leaf_n
    after = (d + 1) % leaf_n
    mate = flip(d, 1)
    lead_row = d - core + 1

    barrier = pltpu.get_barrier_semaphore()
    targets = []
    for t in range(1, 4):
        row = 4 * ((y + t) % 4)
        targets += [on_vec(u) for u in (4 * y + (x + t) % 4, row + x, row + 3 - x)]
    targets += [on_leaf(g) for g in (before, after, flip(d, 2), flip(d, 4))]
    targets += [
        {leaf_axis: mate, vec_axis: vec_of(half * part + (own + t) % part)}
        for t in range(1, part)
    ]
    for target in targets:
        pl.semaphore_signal(
            barrier, inc=1, device_id=target, device_id_type=pl.DeviceIdType.MESH
        )

    mine = [
        pltpu.make_async_copy(pts, ext_pts.at[1], own_sem.at[0]),
        pltpu.make_async_copy(nbr_in, nbr, own_sem.at[1]),
        pltpu.make_async_copy(
            probe,
            ext_probe.at[
                pl.ds(group, group),
                pl.ds(pl.multiple_of(columns * side_row, columns), columns),
            ],
            own_sem.at[2],
        ),
    ]
    quarter = w // 4
    rows = [(0, leaf_inv, w)]
    rows += [(1, local_inv, 2 * quarter + n) for n in range(2)]
    rows += [(1, local_inv, group // 2 + quarter)]
    rows += [(1, local_inv, group - 4 + n) for n in range(3)]
    local_nodes = len(rows)
    offset = 0
    for u in range(1, UPL + 1):
        rows.append((2, upper_inv, offset + d // (1 << u)))
        offset += leaf_n >> u
    inv_copies = [
        pltpu.make_async_copy(source.at[row], inv.at[n], inv_sem.at[n])
        for n, (_, source, row) in enumerate(rows)
    ]
    piv_copies = [
        pltpu.make_async_copy(
            source, piv.at[n, pl.ds(0, source.shape[0])], piv_sem.at[n]
        )
        for n, source in enumerate((leaf_piv, local_piv, upper_piv))
    ]
    for copy in mine[:1] + piv_copies + inv_copies + mine[1:]:
        copy.start()

    def features(side):
        xyz = [ext_pts[side, c].astype(F32) for c in range(3)]
        norm = feature_rows(xyz, 4096.0)
        one = jnp.ones((1, points), F32)
        pad = jnp.zeros((7, points), F32)
        for r in range(group):
            at = [q[r : r + 1] for q in xyz]
            nm = [q[r : r + 1] for q in norm]
            if side == 1:
                near[r] = jnp.concatenate(at + nm + [one] * 3 + [pad], axis=0).astype(BF16)
            rows_far = [q * -8192.0 for q in at] + [one] * 3 + nm + [pad]
            far[side * group + r] = jnp.transpose(
                jnp.concatenate(rows_far, axis=0)
            ).astype(BF16)

    mine[0].wait()
    features(1)

    for copy in piv_copies:
        copy.wait()
    for n, (which, _, row) in enumerate(rows):
        inv_copies[n].wait()
        size = points if n == 0 else 2 * rank
        chosen = piv[which, pl.ds(row, 1), :]
        spread = (
            lax.broadcasted_iota(jnp.int32, (size, rank), 0) == chosen
        ).astype(F32).astype(BF16)
        for m, piece in enumerate(split(jnp.transpose(inv[n]))):
            scattered = mm(piece, spread, NT).astype(BF16)
            if n < local_nodes:
                weights[core, n, m, :, :size] = scattered
            else:
                upper_weights[n - local_nodes, m] = scattered
    mine[1].wait()
    mine[2].wait()

    pl.semaphore_wait(barrier, len(targets))

    def strip(place, row, piece=None):
        start, count = place * group, group
        if piece is not None:
            start, count = start + piece * part, part
        return ext_probe.at[
            pl.ds(start, count), pl.ds(pl.multiple_of(columns * row, columns), columns)
        ]

    ways = [(after, 0), (before, 2)]
    pts_copies = [
        remote(pts, ext_pts.at[place], side_send.at[n], side_recv.at[n], on_leaf(target))
        for n, (target, place) in enumerate(ways)
    ]
    pair_copies = [
        remote(
            probe.at[pl.ds(piece * part, part)],
            strip(1, side_row, piece),
            side_send.at[2 + piece],
            side_recv.at[2 + piece],
            on_vec(flip(v, 1)),
        )
        for piece in range(2)
    ]
    direct = [
        remote(
            probe,
            strip(place, side_row),
            side_send.at[4 + n],
            side_recv.at[4 + n],
            on_leaf(target),
        )
        for n, (target, place) in enumerate(ways)
    ]

    def passed(piece):
        return [
            remote(
                strip(1, 1 - side_row, piece),
                strip(place, 1 - side_row, piece),
                side_send.at[6 + 2 * piece + n],
                side_recv.at[6 + 2 * piece + n],
                on_leaf(target),
            )
            for n, (target, place) in enumerate(ways)
        ]

    for copy in pts_copies + pair_copies + direct:
        copy.start()

    def hand(n, src, dst):
        return remote(src, dst, mate_send.at[n], mate_recv.at[n], on_leaf(mate))

    give_weights = hand(0, weights.at[0], weights.at[0])

    @pl.when(core == 0)
    def _():
        give_weights.start()

    def tile(place, cluster):
        return lax.rsqrt(mm(far[place], near[cluster])).astype(BF16)

    for c in range(part):
        cluster = half * part + c
        tiles[c, :points, :] = tile(group + cluster, cluster)

    pts_copies[0].wait_recv()
    features(0)
    pts_copies[1].wait_recv()
    features(2)

    first = (d - 1) * group

    def place_of(c, k):
        listed = nbr[c, k]
        return jnp.clip(listed - first, 0, 3 * group - 1), listed >= 0

    @pl.loop(0, part)
    def _(c):
        cluster = half * part + c
        for k in range(1, slots):
            place, _ = place_of(cluster, k)
            tiles[c, k * points : (k + 1) * points, :] = tile(place, cluster)
        for piece in range(2):

            @pl.when(c == 2 * piece)
            def _():
                pair_copies[piece].wait_recv()
                for copy in passed(piece):
                    copy.start()

    for copy in direct + passed(0) + passed(1):
        copy.wait_recv()

    z_rows = pl.ds(pl.multiple_of(wide * (2 * y + pair), wide), wide)

    def sketch_copy(t, origin):
        c = half * part + (own + 1 + t) % part
        return remote(
            sketches.at[t],
            z_ref.at[origin, z_rows],
            sk_send.at[t],
            sk_recv.at[origin, t],
            {leaf_axis: lead_row, vec_axis: vec_of(c)},
        )

    last = hand(1, sketches.at[part - 1], z_ref.at[0, z_rows])

    @pl.loop(0, part)
    def _(t):
        c = (own + 1 + t) % part
        for k in range(slots):
            place, listed = place_of(half * part + c, k)
            block = ext_probe[place]
            vectors[:, k * points : (k + 1) * points] = jnp.where(
                listed, block, jnp.zeros_like(block)
            )
        sketches[t] = mm(vectors[...], tiles[c])

        @pl.when(t < part - 1)
        def _():
            sketch_copy(t, core).start()

    def column(q):
        return 2 * (((q + 1) // 2) % 2) + q // 2

    def along(sem, src, dst, step_x, step_y):
        return remote(
            src,
            dst,
            map_send.at[sem],
            map_recv.at[sem],
            on_vec(4 * ((y + step_y) % 4) + (x + step_x) % 4),
        )

    def same(sem, ref, step_x, step_y):
        return along(sem, ref, ref, step_x, step_y)

    steps = (1, 3)
    order = (0, 3, 1, 2)

    def to_x(way):
        return same(16 + way, all_leaf.at[x, :, y], (1, 3, 2)[way], 0)

    def full_y(way, o):
        return same(
            4 * way + o, all_leaf.at[(x + order[o]) % 4, :, y], 0, steps[way]
        )

    def half_y(way, o):
        source = (y + 4 - steps[way]) % 4
        return same(
            8 + 4 * way + o,
            all_leaf.at[(x + order[o]) % 4, way, source],
            0,
            steps[way],
        )

    def local_rows(q, n):
        return pl.ds(2 * column(q), 2) if n == 0 else pl.ds(group // 2 + column(q), 1)

    def full_local(way, n):
        return same(20 + 2 * way + n, all_local.at[:, local_rows(x, n)], steps[way], 0)

    def half_local(way, n):
        source = (x + 4 - steps[way]) % 4
        return same(
            24 + 2 * way + n, all_local.at[way, local_rows(source, n)], steps[way], 0
        )

    give_leaf = hand(2, leaf_map, all_leaf.at[x, :, y])
    give_a = [
        hand(3 + n, maps.at[:, rows_of], all_local.at[:, local_rows(x, n)])
        for n, rows_of in enumerate((pl.ds(0, 2), pl.ds(2, 1)))
    ]
    top_rows = pl.ds(group - 4, 3)
    give_b = hand(5, maps.at[0, pl.ds(3, 3)], out_local.at[top_rows])
    give_upper = [
        hand(6 + u, upper_maps.at[u], out_upper.at[0, u]) for u in range(UPL)
    ]
    give_top = hand(6 + UPL, top_ref, out_top)
    gifts = [give_b] + give_upper + [give_top]
    low_rows = pl.ds(0, group - 4)

    def leaf_columns(n):
        q = (x + n) % 4
        at = pl.ds(4 * column(q), 4)
        return (
            pltpu.make_async_copy(all_leaf.at[q, 0], out_leaf.at[at], out_sem.at[n]),
            hand(7 + UPL + n, all_leaf.at[q, 1], out_leaf.at[at]),
        )

    def low_levels():
        return (
            pltpu.make_async_copy(
                all_local.at[0], out_local.at[low_rows], out_sem.at[4]
            ),
            hand(11 + UPL, all_local.at[1], out_local.at[low_rows]),
        )

    def peer(r, k):
        pos = w % 4 if r == 0 else quarter
        other = flip(pos, k) if k < 3 else 3 - pos
        cluster = 4 * quarter + other if r == 0 else 4 * other + w % 4
        return pos, on_vec(vec_of(cluster))

    def round_copy(r, k):
        pos, target = peer(r, k)
        return remote(
            quad.at[r, pos],
            quad.at[r, pos],
            ex_send.at[3 * r + k - 1],
            ex_recv.at[3 * r + k - 1],
            target,
        )

    def upper_copy(u):
        branch = (d // (1 << u)) % 2
        return remote(
            joined.at[u - 1, branch],
            joined.at[u - 1, branch],
            ex_send.at[5 + u],
            ex_recv.at[5 + u],
            on_leaf(flip(d, 1 << u)),
        )

    def nodes(items):
        parts = [split(zt) for _, zt in items]
        mean_sq = [
            jnp.sum(zt * zt) / (zt.shape[0] * total) + EPSILON for _, zt in items
        ]
        grams = [split(mm3(p, p, NT)) for p in parts]
        return [
            (mm3(scattered, gram) / (total * m), m, p)
            for (scattered, _), gram, m, p in zip(items, grams, mean_sq, parts)
        ]

    def ups(made):
        interps = [split(interp) for interp, _, _ in made]
        return [
            mm3(interp, p) * lax.rsqrt(m) for interp, (_, m, p) in zip(interps, made)
        ]

    def join(left, right):
        return jnp.concatenate([left, right], axis=0)

    def local_weights(g, n):
        return weights[g, n, 0, :, : 2 * rank], weights[g, n, 1, :, : 2 * rank]

    @pl.when(core == 0)
    def _():
        last.start()
        give_leaf.wait_recv()
        for way in range(3):
            to_x(way).start()
        for way in range(2):
            full_y(way, 0).start()
        for came in range(3):
            to_x(came).wait_recv()
            for way in range(2):
                full_y(way, 1 + came).start()
        for way in range(2):
            full_y(way, 0).wait_recv()
            half_y(way, 0).start()
        for copy in give_a:
            copy.wait_recv()
        for way in range(2):
            for n in range(2):
                full_local(way, n).start()
        for o in range(1, 4):
            for way in range(2):
                full_y(way, o).wait_recv()
                half_y(way, o).start()
        for way in range(2):
            for n in range(2):
                full_local(way, n).wait_recv()
                half_local(way, n).start()
        for o in range(4):
            for way in range(2):
                half_y(way, o).wait_recv()
            for copy in leaf_columns(order[o]):
                copy.start()
        for way in range(2):
            for n in range(2):
                half_local(way, n).wait_recv()
        for copy in low_levels():
            copy.start()
        for way in range(3):
            to_x(way).wait_send()
        for way in range(2):
            for o in range(4):
                full_y(way, o).wait_send()
                half_y(way, o).wait_send()
            for n in range(2):
                full_local(way, n).wait_send()
                half_local(way, n).wait_send()
        for local, across in [leaf_columns(n) for n in range(4)] + [low_levels()]:
            local.wait()
            across.wait_send()
        for copy in gifts:
            copy.wait_recv()
        give_weights.wait_send()
        last.wait_send()

    @pl.when(lead)
    def _():
        z_ref[1, z_rows, :] = sketches[part - 1]
        give_weights.wait_recv()

        @pl.loop(0, part - 1)
        def _(t):
            sketch_copy(t, 1).wait_recv()
            sketch_copy(t, 0).wait_recv()

        last.wait_recv()
        pos = w % 4
        made = nodes(
            [
                ((weights[g, 0, 0], weights[g, 0, 1]), jnp.transpose(z_ref[g]))
                for g in range(2)
            ]
        )
        for g in range(2):
            leaf_map[g] = made[g][0]
        give_leaf.start()
        raised = ups(made)
        for g in range(2):
            quad[0, pos, g] = raised[g]
        for r in range(2):
            pos = w % 4 if r == 0 else quarter
            branch = pos // 2
            for k in (1, 3, 2):
                round_copy(r, k).start()
            if r == 1:
                for copy in give_a:
                    copy.start()
            for which, side in ((0, branch), (1, 1 - branch)):
                for k in ((1,), (2, 3))[which]:
                    round_copy(r, k).wait_recv()
                made = nodes(
                    [
                        (
                            local_weights(g, 1 + 3 * r + side),
                            join(quad[r, 2 * side, g], quad[r, 2 * side + 1, g]),
                        )
                        for g in range(2)
                    ]
                )
                raised = ups(made)
                for g in range(2):
                    maps[g, 3 * r + side] = made[g][0]
                    twin[r, side, g] = raised[g]
            made = nodes(
                [
                    (local_weights(g, 3 + 3 * r), join(twin[r, 0, g], twin[r, 1, g]))
                    for g in range(2)
                ]
            )
            raised = ups(made)
            for g in range(2):
                maps[g, 3 * r + 2] = made[g][0]
                if r == 0:
                    quad[1, quarter, g] = raised[g]
        give_b.start()
        own_b = pltpu.make_async_copy(
            maps.at[1, pl.ds(3, 3)], out_local.at[top_rows], out_sem.at[0]
        )
        own_b.start()
        zt = join(*raised)
        own_upper = []
        for u in range(UPL):
            made = nodes([((upper_weights[u, 0], upper_weights[u, 1]), zt)])
            interp, mean_sq, _ = made[0]
            upper_maps[u] = interp
            if u + 1 < UPL:
                joined[u, (d // (2 << u)) % 2] = ups(made)[0]
                upper_copy(u + 1).start()
            give_upper[u].start()
            own_upper.append(
                pltpu.make_async_copy(
                    upper_maps.at[u], out_upper.at[0, u], out_sem.at[1 + u]
                )
            )
            own_upper[-1].start()
            if u + 1 < UPL:
                upper_copy(u + 1).wait_recv()
                zt = join(joined[u, 0], joined[u, 1])
            else:
                z_top[...] = jnp.transpose(zt)
                kept = z_top[pl.ds(pl.multiple_of(v * columns, columns), columns), :]
                top_ref[0] = mm3(split(kept), split(interp), NT) * lax.rsqrt(mean_sq)
        give_top.start()
        own_top = pltpu.make_async_copy(top_ref, out_top, out_sem.at[1 + UPL])
        own_top.start()
        for copy in [own_b, own_top] + own_upper:
            copy.wait()
        for copy in [give_leaf] + give_a + gifts:
            copy.wait_send()
        for r in range(2):
            for k in range(1, 4):
                round_copy(r, k).wait_send()
        for u in range(1, UPL):
            upper_copy(u).wait_send()
        for _, across in [leaf_columns(n) for n in range(4)] + [low_levels()]:
            across.wait_recv()

    @pl.loop(0, part - 1)
    def _(t):
        sketch_copy(t, core).wait_send()

    for copy in pts_copies + pair_copies + direct + passed(0) + passed(1):
        copy.wait_send()


def write_out(a, b, c, e, out_a, out_b, out_c, out_e, buf_a, buf_b, buf_c, buf_e, in_sem, out_sem):
    pieces = []
    for source, buf, target, step in (
        (a, buf_a, out_a, 4),
        (b, buf_b, out_b, 5),
        (c, buf_c, out_c, 1),
        (e, buf_e, out_e, 1),
    ):
        for start in range(0, source.shape[0], step):
            at = pl.ds(start, step)
            n = len(pieces)
            pieces.append(
                (
                    pltpu.make_async_copy(source.at[at], buf.at[at], in_sem.at[n]),
                    pltpu.make_async_copy(buf.at[at], target.at[at], out_sem.at[n]),
                )
            )
    for arrive, _ in pieces:
        arrive.start()
    for arrive, leave in pieces:
        arrive.wait()
        leave.start()
    for _, leave in pieces:
        leave.wait()


def on_device(
    leaf_n,
    vec_n,
    axes,
    points,
    probe_vectors,
    neighbours,
    leaf_pivots,
    leaf_inverse,
    local_pivots,
    local_inverse,
    upper_pivots,
    upper_inverse,
):
    group, columns, size = probe_vectors.shape
    rank = leaf_pivots.shape[1]
    slots = neighbours.shape[1]
    total = columns * vec_n
    part = group // 2
    pivot_rows = max(p.shape[0] for p in (leaf_pivots, local_pivots, upper_pivots))
    anywhere = pl.BlockSpec(memory_space=pl.ANY)
    hbm = pl.BlockSpec(memory_space=pltpu.HBM)
    dma = pltpu.SemaphoreType.DMA
    shapes = (
        jax.ShapeDtypeStruct((group, rank, size), F32),
        jax.ShapeDtypeStruct((group - 1, rank, 2 * rank), F32),
        jax.ShapeDtypeStruct((1, UPL, rank, 2 * rank), F32),
        jax.ShapeDtypeStruct((1, columns, rank), F32),
    )
    made = pl.pallas_call(
        functools.partial(body, leaf_n, vec_n, axes),
        out_shape=shapes,
        in_specs=[hbm] * 9,
        out_specs=[anywhere] * 4,
        scratch_shapes=[
            pltpu.SMEM((group, slots), jnp.int32),
            pltpu.VMEM((3, -(-pivot_rows // 8) * 8, rank), jnp.int32),
            pltpu.VMEM((3, 3, group, size), BF16),
            pltpu.VMEM((3 * group, 2 * columns, size), BF16),
            pltpu.VMEM((group, 16, size), BF16),
            pltpu.VMEM((3 * group, size, 16), BF16),
            pltpu.VMEM((part, slots * size, size), BF16),
            pltpu.VMEM((2 * columns, slots * size), BF16),
            pltpu.VMEM((7 + UPL, rank, rank), F32),
            pltpu.VMEM((2, 7, 2, rank, size), BF16),
            pltpu.VMEM((UPL, 2, rank, 2 * rank), BF16),
            pltpu.VMEM((part, 2 * columns, size), F32),
            pltpu.VMEM((2, total, size), F32),
            pltpu.VMEM((2, 4, 2, rank, total), F32),
            pltpu.VMEM((2, 2, 2, rank, total), F32),
            pltpu.VMEM((UPL - 1, 2, rank, total), F32),
            pltpu.VMEM((total, 2 * rank), F32),
            pltpu.VMEM((2, rank, size), F32),
            pltpu.VMEM((4, 2, 4, rank, size), F32),
            pltpu.VMEM((2, group - 4, rank, 2 * rank), F32),
            pltpu.VMEM((2, 6, rank, 2 * rank), F32),
            pltpu.VMEM((UPL, rank, 2 * rank), F32),
            pltpu.VMEM((1, columns, rank), F32),
            dma((7 + UPL,)),
            dma((3,)),
            dma((3,)),
            dma((10,)),
            dma((10,)),
            dma((part,)),
            dma((2, part)),
            dma((6 + UPL,)),
            dma((6 + UPL,)),
            dma((12 + UPL,)),
            dma((12 + UPL,)),
            dma((28,)),
            dma((28,)),
            dma((5 + UPL,)),
        ],
        compiler_params=pltpu.CompilerParams(
            collective_id=0, has_side_effects=True, vmem_limit_bytes=60 * 2**20
        ),
    )(
        jnp.transpose(points, (1, 0, 2)),
        probe_vectors,
        neighbours,
        leaf_pivots,
        leaf_inverse,
        local_pivots,
        local_inverse,
        upper_pivots,
        upper_inverse,
    )
    leaf_map, local_map, upper_map, top = pl.pallas_call(
        write_out,
        out_shape=shapes,
        in_specs=[anywhere] * 4,
        out_specs=[hbm] * 4,
        scratch_shapes=[pltpu.VMEM(p.shape, p.dtype) for p in shapes] + [dma((9,))] * 2,
        compiler_params=pltpu.CompilerParams(vmem_limit_bytes=60 * 2**20),
    )(*made)
    return (
        jnp.swapaxes(leaf_map, 1, 2),
        jnp.swapaxes(local_map, 1, 2),
        jnp.swapaxes(upper_map, 2, 3),
        top,
    )


def solution(mesh):
    axes = tuple(mesh.axis_names)
    placed = (
        P("leaf", None, None),
        P("leaf", "vec", None),
        P("leaf", None),
        P("leaf", None),
        P("leaf", None, None),
        P("leaf", None),
        P("leaf", None, None),
        P(),
        P(),
    )
    return jax.shard_map(
        functools.partial(on_device, mesh.shape["leaf"], mesh.shape["vec"], axes),
        mesh=mesh,
        in_specs=placed,
        out_specs=(
            P("leaf", None, None),
            P("leaf", None, None),
            P("leaf", None, None, None),
            P("leaf", "vec", None),
        ),
        check_vma=False,
    )
```

```python
import functools

import jax
import jax.numpy as jnp
from jax import lax
from jax.experimental import pallas as pl
from jax.experimental.pallas import tpu as pltpu
from jax.sharding import PartitionSpec as P

UPL = 3
SOFTEN = 0.0009
EPSILON = 1e-06
F32 = jnp.float32
BF16 = jnp.bfloat16
NN = (((1,), (0,)), ((), ()))
NT = (((1,), (1,)), ((), ()))


def mm(a, b, dims=NN):
    return lax.dot_general(a, b, dims, preferred_element_type=F32)


def split(a):
    high = a.astype(BF16)
    return high, (a - high.astype(F32)).astype(BF16)


def mm3(a, b, dims=NN):
    return mm(a[0], b[0], dims) + (mm(a[0], b[1], dims) + mm(a[1], b[0], dims))


def feature_rows(xyz, weight):
    norm = SOFTEN / 2 + xyz[0] * xyz[0] + xyz[1] * xyz[1] + xyz[2] * xyz[2]
    high = norm.astype(BF16).astype(F32)
    rest = norm - high
    middle = rest.astype(BF16).astype(F32)
    low = (rest - middle).astype(BF16).astype(F32)
    return [part * weight for part in (high, middle, low)]


def body(
    leaf_n,
    vec_n,
    axes,
    pts,
    probe,
    nbr_in,
    leaf_piv,
    leaf_inv,
    local_piv,
    local_inv,
    upper_piv,
    upper_inv,
    out_leaf,
    out_local,
    out_upper,
    out_top,
    nbr,
    piv,
    ext_pts,
    ext_probe,
    near,
    far,
    tiles,
    vectors,
    inv,
    weights,
    upper_weights,
    sketches,
    z_ref,
    quad,
    twin,
    joined,
    z_top,
    leaf_map,
    all_leaf,
    all_local,
    maps,
    upper_maps,
    top_ref,
    inv_sem,
    piv_sem,
    own_sem,
    side_send,
    side_recv,
    sk_send,
    sk_recv,
    ex_send,
    ex_recv,
    mate_send,
    mate_recv,
    map_send,
    map_recv,
    out_sem,
):
    leaf_axis, vec_axis = axes
    d = lax.axis_index(leaf_axis)
    v = lax.axis_index(vec_axis)
    group, columns, points = probe.shape
    rank = inv.shape[1]
    total = columns * vec_n
    wide = 2 * columns
    slots = nbr.shape[1]
    part = group // 2

    x, y = v % 4, v // 4
    pair, side_row = x // 2, x % 2
    half = ((x + 1) // 2) % 2
    w = part * half + 4 * pair + y
    own = w % part
    core = d % 2
    lead = core == 1

    def vec_of(cluster):
        high, low = cluster // part, (cluster // 4) % 2
        return 4 * (cluster % 4) + 2 * low + (high + low) % 2

    def on_vec(u):
        return {leaf_axis: d, vec_axis: u}

    def on_leaf(g):
        return {leaf_axis: g, vec_axis: v}

    def remote(src, dst, send, recv, target):
        return pltpu.make_async_remote_copy(
            src_ref=src,
            dst_ref=dst,
            send_sem=send,
            recv_sem=recv,
            device_id=target,
            device_id_type=pl.DeviceIdType.MESH,
        )

    def flip(index, stride):
        return index + stride * (1 - 2 * ((index // stride) % 2))

    before = (d + leaf_n - 1) % leaf_n
    after = (d + 1) % leaf_n
    mate = flip(d, 1)
    lead_row = d - core + 1

    barrier = pltpu.get_barrier_semaphore()
    targets = []
    for t in range(1, 4):
        row = 4 * ((y + t) % 4)
        targets += [on_vec(u) for u in (4 * y + (x + t) % 4, row + x, row + 3 - x)]
    targets += [on_leaf(g) for g in (before, after, flip(d, 2), flip(d, 4))]
    targets += [
        {leaf_axis: mate, vec_axis: vec_of(half * part + (own + t) % part)}
        for t in range(1, part)
    ]
    for target in targets:
        pl.semaphore_signal(
            barrier, inc=1, device_id=target, device_id_type=pl.DeviceIdType.MESH
        )

    mine = [
        pltpu.make_async_copy(pts, ext_pts.at[1], own_sem.at[0]),
        pltpu.make_async_copy(nbr_in, nbr, own_sem.at[1]),
        pltpu.make_async_copy(
            probe,
            ext_probe.at[
                pl.ds(group, group),
                pl.ds(pl.multiple_of(columns * side_row, columns), columns),
            ],
            own_sem.at[2],
        ),
    ]
    quarter = w // 4
    rows = [(0, leaf_inv, w)]
    rows += [(1, local_inv, 2 * quarter + n) for n in range(2)]
    rows += [(1, local_inv, group // 2 + quarter)]
    rows += [(1, local_inv, group - 4 + n) for n in range(3)]
    local_nodes = len(rows)
    offset = 0
    for u in range(1, UPL + 1):
        rows.append((2, upper_inv, offset + d // (1 << u)))
        offset += leaf_n >> u
    inv_copies = [
        pltpu.make_async_copy(source.at[row], inv.at[n], inv_sem.at[n])
        for n, (_, source, row) in enumerate(rows)
    ]
    piv_copies = [
        pltpu.make_async_copy(
            source, piv.at[n, pl.ds(0, source.shape[0])], piv_sem.at[n]
        )
        for n, source in enumerate((leaf_piv, local_piv, upper_piv))
    ]
    for copy in mine[:1] + piv_copies + inv_copies + mine[1:]:
        copy.start()

    def features(side):
        xyz = [ext_pts[side, c].astype(F32) for c in range(3)]
        norm = feature_rows(xyz, 4096.0)
        one = jnp.ones((1, points), F32)
        pad = jnp.zeros((7, points), F32)
        for r in range(group):
            at = [q[r : r + 1] for q in xyz]
            nm = [q[r : r + 1] for q in norm]
            if side == 1:
                near[r] = jnp.concatenate(at + nm + [one] * 3 + [pad], axis=0).astype(BF16)
            rows_far = [q * -8192.0 for q in at] + [one] * 3 + nm + [pad]
            far[side * group + r] = jnp.transpose(
                jnp.concatenate(rows_far, axis=0)
            ).astype(BF16)

    mine[0].wait()
    features(1)

    for copy in piv_copies:
        copy.wait()
    for n, (which, _, row) in enumerate(rows):
        inv_copies[n].wait()
        size = points if n == 0 else 2 * rank
        chosen = piv[which, pl.ds(row, 1), :]
        spread = (
            lax.broadcasted_iota(jnp.int32, (size, rank), 0) == chosen
        ).astype(F32).astype(BF16)
        for m, piece in enumerate(split(jnp.transpose(inv[n]))):
            scattered = mm(piece, spread, NT).astype(BF16)
            if n < local_nodes:
                weights[core, n, m, :, :size] = scattered
            else:
                upper_weights[n - local_nodes, m] = scattered
    mine[1].wait()
    mine[2].wait()

    pl.semaphore_wait(barrier, len(targets))

    def strip(place, row, piece=None):
        start, count = place * group, group
        if piece is not None:
            start, count = start + piece * part, part
        return ext_probe.at[
            pl.ds(start, count), pl.ds(pl.multiple_of(columns * row, columns), columns)
        ]

    ways = [(after, 0), (before, 2)]
    pts_copies = [
        remote(pts, ext_pts.at[place], side_send.at[n], side_recv.at[n], on_leaf(target))
        for n, (target, place) in enumerate(ways)
    ]
    pair_copies = [
        remote(
            probe.at[pl.ds(piece * part, part)],
            strip(1, side_row, piece),
            side_send.at[2 + piece],
            side_recv.at[2 + piece],
            on_vec(flip(v, 1)),
        )
        for piece in range(2)
    ]
    direct = [
        remote(
            probe,
            strip(place, side_row),
            side_send.at[4 + n],
            side_recv.at[4 + n],
            on_leaf(target),
        )
        for n, (target, place) in enumerate(ways)
    ]

    def passed(piece):
        return [
            remote(
                strip(1, 1 - side_row, piece),
                strip(place, 1 - side_row, piece),
                side_send.at[6 + 2 * piece + n],
                side_recv.at[6 + 2 * piece + n],
                on_leaf(target),
            )
            for n, (target, place) in enumerate(ways)
        ]

    for copy in pts_copies + pair_copies + direct:
        copy.start()

    def hand(n, src, dst):
        return remote(src, dst, mate_send.at[n], mate_recv.at[n], on_leaf(mate))

    give_weights = hand(0, weights.at[0], weights.at[0])

    @pl.when(core == 0)
    def _():
        give_weights.start()

    def tile(place, cluster):
        return lax.rsqrt(mm(far[place], near[cluster])).astype(BF16)

    for c in range(part):
        cluster = half * part + c
        tiles[c, :points, :] = tile(group + cluster, cluster)

    pts_copies[0].wait_recv()
    features(0)
    pts_copies[1].wait_recv()
    features(2)

    first = (d - 1) * group

    def place_of(c, k):
        listed = nbr[c, k]
        return jnp.clip(listed - first, 0, 3 * group - 1), listed >= 0

    @pl.loop(0, part)
    def _(c):
        cluster = half * part + c
        for k in range(1, slots):
            place, _ = place_of(cluster, k)
            tiles[c, k * points : (k + 1) * points, :] = tile(place, cluster)
        for piece in range(2):

            @pl.when(c == 2 * piece)
            def _():
                pair_copies[piece].wait_recv()
                for copy in passed(piece):
                    copy.start()

    for copy in direct + passed(0) + passed(1):
        copy.wait_recv()

    z_rows = pl.ds(pl.multiple_of(wide * (2 * y + pair), wide), wide)

    def sketch_copy(t, origin):
        c = half * part + (own + 1 + t) % part
        return remote(
            sketches.at[t],
            z_ref.at[origin, z_rows],
            sk_send.at[t],
            sk_recv.at[origin, t],
            {leaf_axis: lead_row, vec_axis: vec_of(c)},
        )

    last = hand(1, sketches.at[part - 1], z_ref.at[0, z_rows])

    @pl.loop(0, part)
    def _(t):
        c = (own + 1 + t) % part
        for k in range(slots):
            place, listed = place_of(half * part + c, k)
            block = ext_probe[place]
            vectors[:, k * points : (k + 1) * points] = jnp.where(
                listed, block, jnp.zeros_like(block)
            )
        sketches[t] = mm(vectors[...], tiles[c])

        @pl.when(t < part - 1)
        def _():
            sketch_copy(t, core).start()

    def column(q):
        return 2 * (((q + 1) // 2) % 2) + q // 2

    def along(sem, src, dst, step_x, step_y):
        return remote(
            src,
            dst,
            map_send.at[sem],
            map_recv.at[sem],
            on_vec(4 * ((y + step_y) % 4) + (x + step_x) % 4),
        )

    def same(sem, ref, step_x, step_y):
        return along(sem, ref, ref, step_x, step_y)

    steps = (1, 3)
    order = (0, 3, 1, 2)

    def to_x(way):
        return same(16 + way, all_leaf.at[x, :, y], (1, 3, 2)[way], 0)

    def full_y(way, o):
        return same(
            4 * way + o, all_leaf.at[(x + order[o]) % 4, :, y], 0, steps[way]
        )

    def to_far():
        return same(19, all_leaf.at[(x + order[3]) % 4, :, y], 0, 2)

    def half_y(way, o):
        source = (y + 4 - steps[way]) % 4
        return same(
            8 + 4 * way + o,
            all_leaf.at[(x + order[o]) % 4, way, source],
            0,
            steps[way],
        )

    def local_rows(q, n):
        return pl.ds(2 * column(q), 2) if n == 0 else pl.ds(group // 2 + column(q), 1)

    def full_local(way, n):
        return same(20 + 2 * way + n, all_local.at[:, local_rows(x, n)], steps[way], 0)

    def half_local(way, n):
        source = (x + 4 - steps[way]) % 4
        return same(
            24 + 2 * way + n, all_local.at[way, local_rows(source, n)], steps[way], 0
        )

    give_leaf = hand(2, leaf_map, all_leaf.at[x, :, y])
    give_a = [
        hand(3 + n, maps.at[:, rows_of], all_local.at[:, local_rows(x, n)])
        for n, rows_of in enumerate((pl.ds(0, 2), pl.ds(2, 1)))
    ]
    top_rows = pl.ds(group - 4, 3)
    give_b = hand(5, maps.at[0, pl.ds(3, 3)], out_local.at[top_rows])
    give_upper = [
        hand(6 + u, upper_maps.at[u], out_upper.at[0, u]) for u in range(UPL)
    ]
    give_top = hand(6 + UPL, top_ref, out_top)
    gifts = [give_b] + give_upper + [give_top]
    low_rows = pl.ds(0, group - 4)

    def leaf_columns(n):
        q = (x + n) % 4
        at = pl.ds(4 * column(q), 4)
        return (
            pltpu.make_async_copy(all_leaf.at[q, 0], out_leaf.at[at], out_sem.at[n]),
            hand(7 + UPL + n, all_leaf.at[q, 1], out_leaf.at[at]),
        )

    def low_levels():
        return (
            pltpu.make_async_copy(
                all_local.at[0], out_local.at[low_rows], out_sem.at[4]
            ),
            hand(11 + UPL, all_local.at[1], out_local.at[low_rows]),
        )

    def peer(r, k):
        pos = w % 4 if r == 0 else quarter
        other = flip(pos, k) if k < 3 else 3 - pos
        cluster = 4 * quarter + other if r == 0 else 4 * other + w % 4
        return pos, on_vec(vec_of(cluster))

    def round_copy(r, k):
        pos, target = peer(r, k)
        return remote(
            quad.at[r, pos],
            quad.at[r, pos],
            ex_send.at[3 * r + k - 1],
            ex_recv.at[3 * r + k - 1],
            target,
        )

    def upper_copy(u):
        branch = (d // (1 << u)) % 2
        return remote(
            joined.at[u - 1, branch],
            joined.at[u - 1, branch],
            ex_send.at[5 + u],
            ex_recv.at[5 + u],
            on_leaf(flip(d, 1 << u)),
        )

    def nodes(items):
        parts = [split(zt) for _, zt in items]
        mean_sq = [
            jnp.sum(zt * zt) / (zt.shape[0] * total) + EPSILON for _, zt in items
        ]
        grams = [split(mm3(p, p, NT)) for p in parts]
        return [
            (mm3(scattered, gram) / (total * m), m, p)
            for (scattered, _), gram, m, p in zip(items, grams, mean_sq, parts)
        ]

    def ups(made):
        interps = [split(interp) for interp, _, _ in made]
        return [
            mm3(interp, p) * lax.rsqrt(m) for interp, (_, m, p) in zip(interps, made)
        ]

    def join(left, right):
        return jnp.concatenate([left, right], axis=0)

    def local_weights(g, n):
        return weights[g, n, 0, :, : 2 * rank], weights[g, n, 1, :, : 2 * rank]

    @pl.when(core == 0)
    def _():
        last.start()
        give_leaf.wait_recv()
        for way in range(3):
            to_x(way).start()
        for way in range(2):
            full_y(way, 0).start()
        for came in range(3):
            to_x(came).wait_recv()
            for way in range(2):
                full_y(way, 1 + came).start()
        to_far().start()
        for way in range(2):
            full_y(way, 0).wait_recv()
            half_y(way, 0).start()
        for copy in give_a:
            copy.wait_recv()
        for way in range(2):
            for n in range(2):
                full_local(way, n).start()
        for o in range(1, 4):
            for way in range(2):
                full_y(way, o).wait_recv()
                if o < 3:
                    half_y(way, o).start()
        for way in range(2):
            for n in range(2):
                full_local(way, n).wait_recv()
                half_local(way, n).start()
        for o in range(4):
            if o < 3:
                for way in range(2):
                    half_y(way, o).wait_recv()
            else:
                to_far().wait_recv()
            for copy in leaf_columns(order[o]):
                copy.start()
        for way in range(2):
            for n in range(2):
                half_local(way, n).wait_recv()
        for copy in low_levels():
            copy.start()
        for way in range(3):
            to_x(way).wait_send()
        to_far().wait_send()
        for way in range(2):
            for o in range(4):
                full_y(way, o).wait_send()
                if o < 3:
                    half_y(way, o).wait_send()
            for n in range(2):
                full_local(way, n).wait_send()
                half_local(way, n).wait_send()
        for local, across in [leaf_columns(n) for n in range(4)] + [low_levels()]:
            local.wait()
            across.wait_send()
        for copy in gifts:
            copy.wait_recv()
        give_weights.wait_send()
        last.wait_send()

    @pl.when(lead)
    def _():
        z_ref[1, z_rows, :] = sketches[part - 1]
        give_weights.wait_recv()

        @pl.loop(0, part - 1)
        def _(t):
            sketch_copy(t, 1).wait_recv()
            sketch_copy(t, 0).wait_recv()

        last.wait_recv()
        pos = w % 4
        made = nodes(
            [
                ((weights[g, 0, 0], weights[g, 0, 1]), jnp.transpose(z_ref[g]))
                for g in range(2)
            ]
        )
        for g in range(2):
            leaf_map[g] = made[g][0]
        give_leaf.start()
        raised = ups(made)
        for g in range(2):
            quad[0, pos, g] = raised[g]
        for r in range(2):
            pos = w % 4 if r == 0 else quarter
            branch = pos // 2
            for k in (1, 3, 2):
                round_copy(r, k).start()
            if r == 1:
                for copy in give_a:
                    copy.start()
            for which, side in ((0, branch), (1, 1 - branch)):
                for k in ((1,), (2, 3))[which]:
                    round_copy(r, k).wait_recv()
                made = nodes(
                    [
                        (
                            local_weights(g, 1 + 3 * r + side),
                            join(quad[r, 2 * side, g], quad[r, 2 * side + 1, g]),
                        )
                        for g in range(2)
                    ]
                )
                raised = ups(made)
                for g in range(2):
                    maps[g, 3 * r + side] = made[g][0]
                    twin[r, side, g] = raised[g]
            made = nodes(
                [
                    (local_weights(g, 3 + 3 * r), join(twin[r, 0, g], twin[r, 1, g]))
                    for g in range(2)
                ]
            )
            raised = ups(made)
            for g in range(2):
                maps[g, 3 * r + 2] = made[g][0]
                if r == 0:
                    quad[1, quarter, g] = raised[g]
        give_b.start()
        own_b = pltpu.make_async_copy(
            maps.at[1, pl.ds(3, 3)], out_local.at[top_rows], out_sem.at[0]
        )
        own_b.start()
        zt = join(*raised)
        own_upper = []
        for u in range(UPL):
            made = nodes([((upper_weights[u, 0], upper_weights[u, 1]), zt)])
            interp, mean_sq, _ = made[0]
            upper_maps[u] = interp
            if u + 1 < UPL:
                joined[u, (d // (2 << u)) % 2] = ups(made)[0]
                upper_copy(u + 1).start()
            give_upper[u].start()
            own_upper.append(
                pltpu.make_async_copy(
                    upper_maps.at[u], out_upper.at[0, u], out_sem.at[1 + u]
                )
            )
            own_upper[-1].start()
            if u + 1 < UPL:
                upper_copy(u + 1).wait_recv()
                zt = join(joined[u, 0], joined[u, 1])
            else:
                z_top[...] = jnp.transpose(zt)
                kept = z_top[pl.ds(pl.multiple_of(v * columns, columns), columns), :]
                top_ref[0] = mm3(split(kept), split(interp), NT) * lax.rsqrt(mean_sq)
        give_top.start()
        own_top = pltpu.make_async_copy(top_ref, out_top, out_sem.at[1 + UPL])
        own_top.start()
        for copy in [own_b, own_top] + own_upper:
            copy.wait()
        for copy in [give_leaf] + give_a + gifts:
            copy.wait_send()
        for r in range(2):
            for k in range(1, 4):
                round_copy(r, k).wait_send()
        for u in range(1, UPL):
            upper_copy(u).wait_send()
        for _, across in [leaf_columns(n) for n in range(4)] + [low_levels()]:
            across.wait_recv()

    @pl.loop(0, part - 1)
    def _(t):
        sketch_copy(t, core).wait_send()

    for copy in pts_copies + pair_copies + direct + passed(0) + passed(1):
        copy.wait_send()


def write_out(a, b, c, e, out_a, out_b, out_c, out_e, buf_a, buf_b, buf_c, buf_e, in_sem, out_sem):
    pieces = []
    for source, buf, target, step in (
        (a, buf_a, out_a, 4),
        (b, buf_b, out_b, 5),
        (c, buf_c, out_c, 1),
        (e, buf_e, out_e, 1),
    ):
        for start in range(0, source.shape[0], step):
            at = pl.ds(start, step)
            n = len(pieces)
            pieces.append(
                (
                    pltpu.make_async_copy(source.at[at], buf.at[at], in_sem.at[n]),
                    pltpu.make_async_copy(buf.at[at], target.at[at], out_sem.at[n]),
                )
            )
    for arrive, _ in pieces:
        arrive.start()
    for arrive, leave in pieces:
        arrive.wait()
        leave.start()
    for _, leave in pieces:
        leave.wait()


def on_device(
    leaf_n,
    vec_n,
    axes,
    points,
    probe_vectors,
    neighbours,
    leaf_pivots,
    leaf_inverse,
    local_pivots,
    local_inverse,
    upper_pivots,
    upper_inverse,
):
    group, columns, size = probe_vectors.shape
    rank = leaf_pivots.shape[1]
    slots = neighbours.shape[1]
    total = columns * vec_n
    part = group // 2
    pivot_rows = max(p.shape[0] for p in (leaf_pivots, local_pivots, upper_pivots))
    anywhere = pl.BlockSpec(memory_space=pl.ANY)
    hbm = pl.BlockSpec(memory_space=pltpu.HBM)
    dma = pltpu.SemaphoreType.DMA
    shapes = (
        jax.ShapeDtypeStruct((group, rank, size), F32),
        jax.ShapeDtypeStruct((group - 1, rank, 2 * rank), F32),
        jax.ShapeDtypeStruct((1, UPL, rank, 2 * rank), F32),
        jax.ShapeDtypeStruct((1, columns, rank), F32),
    )
    made = pl.pallas_call(
        functools.partial(body, leaf_n, vec_n, axes),
        out_shape=shapes,
        in_specs=[hbm] * 9,
        out_specs=[anywhere] * 4,
        scratch_shapes=[
            pltpu.SMEM((group, slots), jnp.int32),
            pltpu.VMEM((3, -(-pivot_rows // 8) * 8, rank), jnp.int32),
            pltpu.VMEM((3, 3, group, size), BF16),
            pltpu.VMEM((3 * group, 2 * columns, size), BF16),
            pltpu.VMEM((group, 16, size), BF16),
            pltpu.VMEM((3 * group, size, 16), BF16),
            pltpu.VMEM((part, slots * size, size), BF16),
            pltpu.VMEM((2 * columns, slots * size), BF16),
            pltpu.VMEM((7 + UPL, rank, rank), F32),
            pltpu.VMEM((2, 7, 2, rank, size), BF16),
            pltpu.VMEM((UPL, 2, rank, 2 * rank), BF16),
            pltpu.VMEM((part, 2 * columns, size), F32),
            pltpu.VMEM((2, total, size), F32),
            pltpu.VMEM((2, 4, 2, rank, total), F32),
            pltpu.VMEM((2, 2, 2, rank, total), F32),
            pltpu.VMEM((UPL - 1, 2, rank, total), F32),
            pltpu.VMEM((total, 2 * rank), F32),
            pltpu.VMEM((2, rank, size), F32),
            pltpu.VMEM((4, 2, 4, rank, size), F32),
            pltpu.VMEM((2, group - 4, rank, 2 * rank), F32),
            pltpu.VMEM((2, 6, rank, 2 * rank), F32),
            pltpu.VMEM((UPL, rank, 2 * rank), F32),
            pltpu.VMEM((1, columns, rank), F32),
            dma((7 + UPL,)),
            dma((3,)),
            dma((3,)),
            dma((10,)),
            dma((10,)),
            dma((part,)),
            dma((2, part)),
            dma((6 + UPL,)),
            dma((6 + UPL,)),
            dma((12 + UPL,)),
            dma((12 + UPL,)),
            dma((28,)),
            dma((28,)),
            dma((5 + UPL,)),
        ],
        compiler_params=pltpu.CompilerParams(
            collective_id=0, has_side_effects=True, vmem_limit_bytes=60 * 2**20
        ),
    )(
        jnp.transpose(points, (1, 0, 2)),
        probe_vectors,
        neighbours,
        leaf_pivots,
        leaf_inverse,
        local_pivots,
        local_inverse,
        upper_pivots,
        upper_inverse,
    )
    leaf_map, local_map, upper_map, top = pl.pallas_call(
        write_out,
        out_shape=shapes,
        in_specs=[anywhere] * 4,
        out_specs=[hbm] * 4,
        scratch_shapes=[pltpu.VMEM(p.shape, p.dtype) for p in shapes] + [dma((9,))] * 2,
        compiler_params=pltpu.CompilerParams(vmem_limit_bytes=60 * 2**20),
    )(*made)
    return (
        jnp.swapaxes(leaf_map, 1, 2),
        jnp.swapaxes(local_map, 1, 2),
        jnp.swapaxes(upper_map, 2, 3),
        top,
    )


def solution(mesh):
    axes = tuple(mesh.axis_names)
    placed = (
        P("leaf", None, None),
        P("leaf", "vec", None),
        P("leaf", None),
        P("leaf", None),
        P("leaf", None, None),
        P("leaf", None),
        P("leaf", None, None),
        P(),
        P(),
    )
    return jax.shard_map(
        functools.partial(on_device, mesh.shape["leaf"], mesh.shape["vec"], axes),
        mesh=mesh,
        in_specs=placed,
        out_specs=(
            P("leaf", None, None),
            P("leaf", None, None),
            P("leaf", None, None, None),
            P("leaf", "vec", None),
        ),
        check_vma=False,
    )
```
